32 devices in a mesh: dp: 4 (over z), hidden: 8 (over y, x, core).
Axes of the slice: x: 2, y: 2, z: 4, core: 2. Of those that a mesh axis runs over, the one named last changes fastest.
Arguments:
- tokens: bfloat16 [128, 4096], P('dp', 'hidden'), may hold values from -6 to 6
- grad_out: bfloat16 [128, 4096], P('dp', 'hidden'), may hold values from -6 to 6
- routes: int32 [128, 2], P('dp'), may hold values from 0 to 3, all different within a row; in each aligned block of 32 rows (0 to 31, 32 to 63, ...) at most 20 rows name the same one
- probs: bfloat16 [128, 2], P('dp'), may hold values from 0.099609375 to 0.8984375
- gate_weight: bfloat16 [28672, 4096], P(('dp', 'hidden')), may hold values from -0.09375 to 0.09375
- up_weight: bfloat16 [28672, 4096], P(('dp', 'hidden')), may hold values from -0.09375 to 0.09375
- down_weight: bfloat16 [28672, 4096], P(('dp', 'hidden')), may hold values from -0.0625 to 0.0625
Outputs:
- grad_tokens: bfloat16 [128, 4096], P('dp', 'hidden')
- grad_probs: float32 [128, 2], P('dp')
- grad_gate: bfloat16 [28672, 4096], P(('dp', 'hidden'))
- grad_up: bfloat16 [28672, 4096], P(('dp', 'hidden'))
The draws below stay inside these ranges and needn't reach their ends.
Inputs may be any that keep to these rules, and one draw needn't show every extreme that they name: `routes`: A token's two experts differ. Among the 32 tokens of one index of dp no expert is named more than 20 times, a bound that some block reaches.
All inputs are finite; a program needn't handle non-finite values.
Results may differ from the reference program's by a relative error of at most 0.0049.
Values may be sent and summed in bfloat16 or wider, within the bound.
A program may use at most 128 MiB of HBM per device.

```python
import math
import jax
import jax.numpy as jnp
import numpy as np

D = 4096
FB = 7168
TOK_DEV = 32
CAP = 20
EXPERTS = 4
TOKENS = 128
N_DP = 4


def block_levels(key, dims, cuts, smallest, high):
    gain = 1.0
    for position, blocks in cuts:
        steps = jax.random.uniform(jax.random.fold_in(jax.random.fold_in(key, 6), position), (blocks,), jnp.float32, smallest / len(cuts), high / len(cuts))
        gain = gain * jnp.repeat(jnp.exp(steps), dims[position] // blocks).reshape((-1,) + (1,) * (len(dims) - 1 - position))
    return gain


def assign_block(key, own, number, rows, count, top, limit, slope):
    order = jax.random.permutation(key, count)
    heavy_load, usual = portions_of(count, rows * top, limit, slope, True), portions_of(count, rows * top, limit, slope, False)
    places = jnp.arange(count)

    def named(tallies, turn):
        used = int((tallies > 0).sum())
        fixed = max(1, used // 4)
        passed = fixed + (places - fixed + turn * (used - fixed)) % max(1, count - fixed)
        return jnp.zeros((count,), jnp.int32).at[order[jnp.where(places < fixed, places, passed)]].set(jnp.asarray(tallies, jnp.int32))

    tallies = jnp.where(number % 4 == 0, named(heavy_load, number // 4), named(usual, number - number // 4 - 1))
    mixed = jax.random.permutation(jax.random.fold_in(own, 3), count)
    source_of, receiver = mixed[0:count // 2 * 2:2], mixed[1:count // 2 * 2:2]
    slack = jnp.minimum(tallies[source_of] - 1, limit - tallies[receiver]) // 2
    slack = jnp.where((source_of == order[0]) | (receiver == order[0]) | (tallies[receiver] == 0), 0, jnp.maximum(slack, 0))
    passed = jax.random.randint(jax.random.fold_in(own, 4), (count // 2,), 0, 1 << 20) % (slack + 1)
    tallies = tallies.at[source_of].add(-passed).at[receiver].add(passed)
    members = jnp.searchsorted(jnp.cumsum(tallies), jnp.arange(rows * top), side="right").astype(jnp.int32)
    grid = members.reshape(top, rows).T
    grid = grid[jax.random.permutation(jax.random.fold_in(own, 1), rows)]
    turn = jax.random.randint(jax.random.fold_in(own, 2), (rows, 1), 0, top)
    return jnp.take_along_axis(grid, (jnp.arange(top)[None, :] + turn) % top, axis=1)


def portions_of(amount, total, bound, slope, full):
    portions = [(1 << 20) // math.isqrt(rank ** slope) + 1 for rank in range(1, amount + 1)]
    largest = bound if full else min(bound, max(-(-total // amount), total * portions[0] // sum(portions)))
    least = 1 if total - largest >= amount - 1 else 0
    given, surplus = [largest] + [least] * (amount - 1), total - largest - least * (amount - 1)
    while surplus > 0:
        free = [i for i in range(1, amount) if given[i] < largest] or [i for i in range(1, amount) if given[i] < bound]
        pool, budget = sum([portions[i] for i in free]), surplus
        for i in free:
            extra = min(bound - given[i], max(1, budget * portions[i] // pool), surplus)
            given[i] = given[i] + extra
            surplus = surplus - extra
    return np.array(given)


def normal_values(key, shape, scale, bound, pieces=(), held_as=jnp.bfloat16):
    entries = scale * jax.random.normal(key, shape, jnp.float32)
    if pieces:
        entries = entries * block_levels(key, shape, pieces, -0.22, 0.18)
    return jnp.clip(entries, -bound, bound).astype(held_as)


def setup_inputs(seed: int = 0) -> dict:
    key_list = jax.random.split(jax.random.key(seed), 8)
    tokens = normal_values(key_list[0], (TOKENS, D), 1.0, 6.0, ((0, 4), (1, 8)))
    grad_out = normal_values(key_list[1], (TOKENS, D), 1.0, 6.0, ((0, 4), (1, 8)))
    routes_keys = jax.random.split(jax.random.fold_in(key_list[2], 1), TOKENS // TOK_DEV)
    routes_turns = jax.random.permutation(jax.random.fold_in(key_list[2], 3), TOKENS // TOK_DEV)
    routes = jax.vmap(lambda own, number: assign_block(jax.random.fold_in(key_list[2], 2), own, number, TOK_DEV, EXPERTS, 2, CAP, 2))(routes_keys, routes_turns).reshape((TOKENS, 2))
    probs = jnp.clip(0.099609375 + 0.7988281 * jax.random.uniform(key_list[3], (TOKENS, 2), jnp.float32) ** block_levels(key_list[3], (TOKENS, 2), ((0, 4),), -0.2, 0.2), 0.099609375, 0.8984375).astype(jnp.bfloat16)
    gate_weight = normal_values(key_list[4], (N_DP * FB, D), D ** -0.5, 0.09375, ((0, 32),))
    up_weight = normal_values(key_list[5], (N_DP * FB, D), D ** -0.5, 0.09375, ((0, 32),))
    down_weight = normal_values(key_list[6], (N_DP * FB, D), FB ** -0.5, 0.0625, ((0, 32),))
    return dict(tokens=tokens, grad_out=grad_out, routes=routes, probs=probs, gate_weight=gate_weight, up_weight=up_weight, down_weight=down_weight)


def reference(tokens, grad_out, routes, probs, gate_weight, up_weight, down_weight):
    large_count = N_DP // 6
    weights_f = probs.astype(jnp.float32)
    grad_total = jnp.zeros((TOKENS, D), jnp.float32)
    grad_router = jnp.zeros((TOKENS, 2), jnp.float32)
    gate_grads = []
    up_grads = []
    for block_index in range(N_DP):
        if block_index < 4 * large_count:
            expert_id = block_index // 4
        else:
            expert_id = block_index - 3 * large_count
        first = block_index * FB
        gate_rows = gate_weight[first:first + FB]
        up_rows = up_weight[first:first + FB]
        down_rows = down_weight[first:first + FB]
        matched = routes == expert_id
        block_prob = jnp.sum(jnp.where(matched, weights_f, 0.0), axis=1)
        gate_pre = jnp.dot(tokens, gate_rows.T, preferred_element_type=jnp.float32)
        up_pre = jnp.dot(tokens, up_rows.T, preferred_element_type=jnp.float32)
        back_pre = jnp.dot(grad_out, down_rows.T, preferred_element_type=jnp.float32)
        sigmoid_gate = jax.nn.sigmoid(gate_pre)
        silu_gate = gate_pre * sigmoid_gate
        router_part = jnp.sum(silu_gate * up_pre * back_pre, axis=1)
        scaled = block_prob[:, None] * back_pre
        grad_gate_pre = (scaled * up_pre * sigmoid_gate * (1.0 + gate_pre * (1.0 - sigmoid_gate))).astype(jnp.bfloat16)
        grad_up_pre = (scaled * silu_gate).astype(jnp.bfloat16)
        gate_grads.append(jnp.dot(grad_gate_pre.T, tokens, preferred_element_type=jnp.float32).astype(jnp.bfloat16))
        up_grads.append(jnp.dot(grad_up_pre.T, tokens, preferred_element_type=jnp.float32).astype(jnp.bfloat16))
        grad_total = grad_total + jnp.dot(grad_gate_pre, gate_rows, preferred_element_type=jnp.float32)
        grad_total = grad_total + jnp.dot(grad_up_pre, up_rows, preferred_element_type=jnp.float32)
        grad_router = grad_router + jnp.where(matched, router_part[:, None], 0.0)
    return (grad_total.astype(jnp.bfloat16), grad_router, jnp.concatenate(gate_grads, axis=0), jnp.concatenate(up_grads, axis=0))
```

```python
import functools

import jax
import jax.numpy as jnp
from jax import lax
from jax.experimental import pallas as pl
from jax.experimental.pallas import tpu as pltpu
from jax.sharding import PartitionSpec as P

CAP = 20


def body(tokens, grad_out, routes, probs, gate_weight, up_weight, down_weight):
    dp_count = lax.axis_size("dp")
    hidden_count = lax.axis_size("hidden")
    large_count = dp_count // 6
    expert_total = dp_count - 3 * large_count
    block_ids = jnp.arange(dp_count, dtype=jnp.int32)
    owners = jnp.where(block_ids < 4 * large_count, block_ids // 4, block_ids - 3 * large_count)
    expert_hits = (
        routes[:, :, None] == jnp.arange(expert_total, dtype=jnp.int32)[None, None, :]
    ).astype(jnp.int32)
    per_token = jnp.sum(expert_hits, axis=1)
    before = jnp.cumsum(per_token, axis=0) - per_token
    slot_rank = jnp.sum(expert_hits * before[:, None, :], axis=2)
    matches = routes[:, :, None] == owners[None, None, :]
    slot_hits = slot_rank[:, :, None, None] == jnp.arange(CAP, dtype=jnp.int32)[None, None, None, :]
    picked = (matches[:, :, :, None] & slot_hits).astype(jnp.float32)
    select = jnp.sum(picked, axis=1)
    select_half = select.astype(jnp.bfloat16)
    send_tokens = jnp.einsum(
        "tjc,td->jcd", select_half, tokens, preferred_element_type=jnp.float32
    ).astype(jnp.bfloat16)
    send_grads = jnp.einsum(
        "tjc,td->jcd", select_half, grad_out, preferred_element_type=jnp.float32
    ).astype(jnp.bfloat16)
    send_probs = jnp.einsum(
        "tkjc,tk->jc", picked, probs.astype(jnp.float32), precision=lax.Precision.HIGHEST
    ).astype(jnp.bfloat16)
    recv_tokens, recv_grads, recv_probs = (
        lax.all_to_all(send_tokens, "dp", split_axis=0, concat_axis=0, tiled=True),
        lax.all_to_all(send_grads, "dp", split_axis=0, concat_axis=0, tiled=True),
        lax.all_to_all(send_probs, "dp", split_axis=0, concat_axis=0, tiled=True),
    )
    row_count = dp_count * CAP
    contract = (((1,), (1,)), ((), ()))
    full_tokens, full_grads = (
        lax.all_gather(recv_tokens, "hidden", axis=2, tiled=True),
        lax.all_gather(recv_grads, "hidden", axis=2, tiled=True),
    )
    token_rows = full_tokens.reshape(row_count, full_tokens.shape[2])
    grad_rows = full_grads.reshape(row_count, full_grads.shape[2])
    back_pre = lax.dot_general(grad_rows, down_weight, contract, preferred_element_type=jnp.float32)
    slot_probs = recv_probs.reshape(row_count).astype(jnp.float32)
    gate_pre = lax.dot_general(
        token_rows, gate_weight, contract, preferred_element_type=jnp.float32
    )
    up_pre = lax.dot_general(token_rows, up_weight, contract, preferred_element_type=jnp.float32)
    sigmoid_gate = jax.nn.sigmoid(gate_pre)
    silu_gate = gate_pre * sigmoid_gate
    router_part = jnp.sum(silu_gate * up_pre * back_pre, axis=1)
    scaled = slot_probs[:, None] * back_pre
    grad_gate_pre = (
        scaled * up_pre * sigmoid_gate * (1.0 + gate_pre * (1.0 - sigmoid_gate))
    ).astype(jnp.bfloat16)
    grad_up_pre = (scaled * silu_gate).astype(jnp.bfloat16)
    over_rows = (((0,), (0,)), ((), ()))
    grad_gate = lax.dot_general(
        grad_gate_pre, token_rows, over_rows, preferred_element_type=jnp.float32
    ).astype(jnp.bfloat16)
    grad_up = lax.dot_general(
        grad_up_pre, token_rows, over_rows, preferred_element_type=jnp.float32
    ).astype(jnp.bfloat16)
    feature_width = gate_weight.shape[1] // hidden_count
    cross = (((0,), (1,)), ((), ()))
    own_features = lax.psum_scatter(
        lax.dot_general(gate_weight, grad_gate_pre, cross, preferred_element_type=jnp.float32)
        + lax.dot_general(up_weight, grad_up_pre, cross, preferred_element_type=jnp.float32),
        "hidden",
        scatter_dimension=0,
        tiled=True,
    ).T
    router_payload = lax.psum(router_part, "hidden")
    back_features, back_router = (
        lax.all_to_all(
            own_features.reshape(dp_count, CAP, feature_width),
            "dp",
            split_axis=0,
            concat_axis=0,
            tiled=True,
        ),
        lax.all_to_all(
            router_payload.reshape(dp_count, CAP), "dp", split_axis=0, concat_axis=0, tiled=True
        ),
    )
    token_router = jnp.einsum("tkjc,jc->tk", picked, back_router, precision=lax.Precision.HIGHEST)
    grad_tokens = jnp.einsum(
        "tjc,jcd->td", select, back_features, precision=lax.Precision.HIGHEST
    ).astype(jnp.bfloat16)
    return (grad_tokens, token_router, grad_gate, grad_up)


LANES = 128
MESH = pl.DeviceIdType.MESH
F32 = jnp.float32
BF16 = jnp.bfloat16
NT = (((1,), (1,)), ((), ()))
NN = (((1,), (0,)), ((), ()))
TN = (((0,), (0,)), ((), ()))


def fits(dp_count, hidden_count, token_shape, weight_shape):
    rows, width = token_shape
    groups = width // LANES
    return (
        hidden_count == 8
        and 2 <= dp_count <= 8
        and width % LANES == 0
        and rows * groups == LANES
        and (CAP * groups) % 16 == 0
        and (CAP * dp_count) % 16 == 0
        and CAP * dp_count <= LANES
        and weight_shape[0] % LANES == 0
    )


def dot(a, b, dims):
    return lax.dot_general(a, b, dims, preferred_element_type=F32)


def steps_of(values, size, count):
    total = jnp.zeros_like(values)
    for edge in range(1, count):
        total = total + (values >= edge * size).astype(jnp.int32)
    return total


def fused_kernel(
    dp_count,
    owners,
    routes_ref,
    probs_ref,
    tokens_ref,
    grads_ref,
    gate_hbm,
    up_hbm,
    down_hbm,
    grad_tokens_ref,
    grad_probs_ref,
    x_out,
    d_out,
    weights,
    weight_sem,
    xbuf,
    x_send,
    x_recv,
    zsend,
    zrecv,
    z_send_sem,
    z_recv_sem,
    aux_send,
    aux_recv,
    aux_send_sem,
    aux_recv_sem,
    acc,
    dbuf,
    one_send,
    one_recv,
    one_send_sem,
    one_recv_sem,
    two_send,
    two_recv,
    two_send_sem,
    two_recv_sem,
    own_part,
    q_send,
    q_recv,
    q_send_sem,
    q_recv_sem,
    back_send,
    back_recv,
    back_send_sem,
    back_recv_sem,
    qz_send,
    qz_recv,
    qz_send_sem,
    qz_recv_sem,
    out_sem,
):
    rows, width = tokens_ref.shape
    groups = width // LANES
    packed = CAP * groups
    slots = CAP * dp_count
    plane = lax.axis_index("dp")
    h = lax.axis_index("hidden")
    core = h % 2
    x_pos = (h // 2) % 2
    y_pos = h // 4
    to_sib = 1 - 2 * core
    sib = h + to_sib
    hx = h + 2 - 4 * x_pos
    hy = h + 4 - 8 * y_pos
    hd = hx + 4 - 8 * y_pos

    def at_hidden(index):
        return (plane, index)

    def at_plane(step):
        other = (plane + step) % dp_count
        return other, (other, h)

    barrier = pltpu.get_barrier_semaphore()
    for index in (sib, hx, hy, hd):
        pl.semaphore_signal(barrier, inc=1, device_id=at_hidden(index), device_id_type=MESH)
    for step in range(1, dp_count):
        pl.semaphore_signal(barrier, inc=1, device_id=at_plane(step)[1], device_id_type=MESH)

    order = (h, sib, hx, hy, hx + to_sib, hy + to_sib, hd, hd + to_sib)

    def weight_copy(which, index):
        columns = pl.ds(pl.multiple_of(index * width, width), width)
        source = (gate_hbm, up_hbm, down_hbm)[which]
        return pltpu.make_async_copy(
            source.at[:, columns], weights.at[which, index], weight_sem.at[which, index]
        )

    for index in order:
        for which in range(3):
            weight_copy(which, index).start()

    pending = []

    def send(source, target, send_sem, recv_sem, device):
        copy = pltpu.make_async_remote_copy(
            src_ref=source,
            dst_ref=target,
            send_sem=send_sem,
            recv_sem=recv_sem,
            device_id=device,
            device_id_type=MESH,
        )
        copy.start()
        pending.append(copy)

    def arrived(target, send_sem, recv_sem):
        pltpu.make_async_remote_copy(
            src_ref=target,
            dst_ref=target,
            send_sem=send_sem,
            recv_sem=recv_sem,
            device_id=at_hidden(sib),
            device_id_type=MESH,
        ).wait_recv()

    block_row = lax.broadcasted_iota(jnp.int32, (8, rows), 0)
    owner_of = jnp.full((8, rows), -1, jnp.int32)
    for j, owner in enumerate(owners):
        owner_of = jnp.where(block_row == j, owner, owner_of)
    first = jnp.broadcast_to(routes_ref[0:1, :], (8, rows))
    second = jnp.broadcast_to(routes_ref[1:2, :], (8, rows))
    prob_rows = probs_ref[...].astype(F32)
    match = (owner_of == first) | (owner_of == second)
    earlier = lax.broadcasted_iota(jnp.int32, (rows, rows), 0) < lax.broadcasted_iota(
        jnp.int32, (rows, rows), 1
    )
    rank = dot(match.astype(F32).astype(BF16), earlier.astype(F32).astype(BF16), NN)
    rank = jnp.where(match, rank, -1.0)
    block_prob = jnp.where(owner_of == first, jnp.broadcast_to(prob_rows[0:1, :], (8, rows)), 0.0)
    block_prob = block_prob + jnp.where(
        owner_of == second, jnp.broadcast_to(prob_rows[1:2, :], (8, rows)), 0.0
    )
    for j in range(dp_count):
        aux_send[j] = jnp.zeros((8, LANES), F32)
        aux_send[j, 0:1, 0:rows] = rank[j : j + 1, :]
        aux_send[j, 1:2, 0:rows] = block_prob[j : j + 1, :]
    wide_rank = jnp.concatenate([rank] * groups, axis=1)
    pack_row = lax.broadcasted_iota(jnp.int32, (packed, LANES), 0)
    pack_group = steps_of(pack_row, CAP, groups)
    pack_slot = (pack_row - CAP * pack_group).astype(F32)
    lane_group = steps_of(lax.broadcasted_iota(jnp.int32, (packed, LANES), 1), rows, groups)
    same_group = pack_group == lane_group
    select = jnp.concatenate(
        [
            jnp.where(
                same_group & (pack_slot == jnp.broadcast_to(wide_rank[j : j + 1, :], pack_slot.shape)),
                1.0,
                0.0,
            )
            for j in range(dp_count)
        ],
        axis=0,
    ).astype(BF16)

    for a, ref in enumerate((tokens_ref, grads_ref)):
        stacked = jnp.concatenate(
            [ref[:, n * LANES : (n + 1) * LANES] for n in range(groups)], axis=0
        )
        zsend[a] = dot(select, stacked, NN).astype(BF16).reshape(dp_count, packed, LANES)
        zrecv[a, plane] = zsend[a, plane]
        if a == 0:
            aux_recv[plane] = aux_send[plane]
            pl.semaphore_wait(barrier, 4 + dp_count - 1)
        for step in range(1, dp_count):
            other, device = at_plane(step)
            send(
                zsend.at[a, other],
                zrecv.at[a, plane],
                z_send_sem.at[a, step],
                z_recv_sem.at[a, plane],
                device,
            )
    for step in range(1, dp_count):
        other, device = at_plane(step)
        send(
            aux_send.at[other],
            aux_recv.at[plane],
            aux_send_sem.at[step],
            aux_recv_sem.at[plane],
            device,
        )

    def shift_of(shape, axis):
        slot = lax.broadcasted_iota(jnp.int32, shape, axis)
        return slot, slot + (packed - CAP) * steps_of(slot, CAP, dp_count)

    slot_index, slot_base = shift_of((slots, dp_count * packed), 0)
    packed_index = lax.broadcasted_iota(jnp.int32, (slots, dp_count * packed), 1)
    unpack = [
        jnp.where(packed_index == slot_base + CAP * n, 1.0, 0.0).astype(BF16) for n in range(groups)
    ]
    for a in range(2):
        for step in range(1, dp_count):
            other = (plane + step) % dp_count
            arrived(zrecv.at[a, other], z_send_sem.at[a, step], z_recv_sem.at[a, other])
        received = zrecv[a].reshape(dp_count * packed, LANES)
        for n in range(groups):
            xbuf[a, h, :, n * LANES : (n + 1) * LANES] = dot(unpack[n], received, NN).astype(BF16)
        for slot, partner in enumerate((hx, hy, sib)):
            send(
                xbuf.at[a, h],
                xbuf.at[a, h],
                x_send.at[a, slot],
                x_recv.at[a, h],
                at_hidden(partner),
            )

    def wait_x(a, index):
        arrived(xbuf.at[a, index], x_send.at[a, 0], x_recv.at[a, index])

    def forward(a, index, partner, slot):
        send(
            xbuf.at[a, index],
            xbuf.at[a, index],
            x_send.at[a, slot],
            x_recv.at[a, index],
            at_hidden(partner),
        )

    def project(which, index, start):
        weight_copy(which, index).wait()
        part = dot(xbuf[0 if which < 2 else 1, index], weights[which, index], NT)
        acc[which] = part if start else acc[which] + part

    def project_all(index):
        for which in range(3):
            project(which, index, False)

    project(0, h, True)
    project(1, h, True)
    wait_x(0, hx)
    forward(0, hx, hy, 3)
    forward(0, hx, sib, 4)
    wait_x(0, hy)
    forward(0, hy, sib, 5)
    project(2, h, True)
    wait_x(1, hy)
    forward(1, hy, hx, 3)
    forward(1, hy, sib, 4)
    wait_x(1, hx)
    forward(1, hx, sib, 5)
    wait_x(0, sib)
    wait_x(1, sib)
    project_all(sib)
    project_all(hx)
    wait_x(0, hd)
    forward(0, hd, sib, 6)
    wait_x(1, hd)
    forward(1, hd, sib, 6)
    project_all(hy)
    for index in (hx + to_sib, hy + to_sib):
        wait_x(0, index)
        wait_x(1, index)
        project_all(index)
    project_all(hd)
    wait_x(0, hd + to_sib)
    wait_x(1, hd + to_sib)
    project_all(hd + to_sib)
    x_copy = pltpu.make_async_copy(xbuf.at[0], x_out, out_sem.at[0])
    x_copy.start()

    for step in range(1, dp_count):
        other = (plane + step) % dp_count
        arrived(aux_recv.at[other], aux_send_sem.at[step], aux_recv_sem.at[other])
    slot_value = lax.broadcasted_iota(jnp.int32, (slots, rows), 0).astype(F32)
    slot_prob = jnp.zeros((slots, 1), F32)
    for source in range(dp_count):
        source_rank = jnp.broadcast_to(aux_recv[source, 0:1, 0:rows], (slots, rows))
        source_prob = jnp.broadcast_to(aux_recv[source, 1:2, 0:rows], (slots, rows))
        hit = (source_rank >= 0.0) & (slot_value == source_rank + float(CAP * source))
        slot_prob = slot_prob + jnp.sum(jnp.where(hit, source_prob, 0.0), axis=1, keepdims=True)

    gate_pre = acc[0]
    up_pre = acc[1]
    back_pre = acc[2]
    sigmoid_gate = jax.nn.sigmoid(gate_pre)
    silu_gate = gate_pre * sigmoid_gate
    scaled = slot_prob * back_pre
    dbuf[0] = (scaled * up_pre * sigmoid_gate * (1.0 + gate_pre * (1.0 - sigmoid_gate))).astype(BF16)
    dbuf[1] = (scaled * silu_gate).astype(BF16)
    router = jnp.sum(silu_gate * up_pre * back_pre, axis=1, keepdims=True)
    d_copy = pltpu.make_async_copy(dbuf, d_out, out_sem.at[1])
    d_copy.start()

    def row_of(column):
        tall = jnp.concatenate(
            [jnp.broadcast_to(column, (slots, LANES)), jnp.zeros((LANES - slots, LANES), F32)], axis=0
        )
        return tall.T[0:8, :]

    q_send[0] = row_of(router)
    send(q_send.at[0], q_recv.at[0], q_send_sem.at[0], q_recv_sem.at[0], at_hidden(sib))

    def partial(index):
        return dot(dbuf[0], weights[0, index], NN) + dot(dbuf[1], weights[1, index], NN)

    for slot, index in enumerate((hd, hx, hy, h)):
        one_send[slot] = partial(index + to_sib).astype(BF16)
        send(
            one_send.at[slot],
            one_recv.at[slot],
            one_send_sem.at[slot],
            one_recv_sem.at[slot],
            at_hidden(sib),
        )
    arrived(q_recv.at[0], q_send_sem.at[0], q_recv_sem.at[0])
    q_send[1] = q_send[0] + q_recv[0]
    for slot, index in enumerate((hd, hx, hy)):
        send(
            q_send.at[1],
            q_recv.at[1 + slot],
            q_send_sem.at[1 + slot],
            q_recv_sem.at[1 + slot],
            at_hidden(index),
        )
    for slot, index in enumerate((hd, hx, hy, h)):
        own = partial(index)
        arrived(one_recv.at[slot], one_send_sem.at[slot], one_recv_sem.at[slot])
        total = own + one_recv[slot].astype(F32)
        if slot == 3:
            own_part[...] = total
        else:
            two_send[slot] = total.astype(BF16)
            send(
                two_send.at[slot],
                two_recv.at[slot],
                two_send_sem.at[slot],
                two_recv_sem.at[slot],
                at_hidden(index),
            )

    for slot in range(3):
        arrived(q_recv.at[1 + slot], q_send_sem.at[1 + slot], q_recv_sem.at[1 + slot])
    q_total = (q_send[1] + q_recv[2]) + (q_recv[3] + q_recv[1])
    qz_send[...] = q_total
    qz_recv[plane] = q_total
    for step in range(1, dp_count):
        _, device = at_plane(step)
        send(qz_send, qz_recv.at[plane], qz_send_sem.at[step], qz_recv_sem.at[plane], device)

    for slot in range(3):
        arrived(two_recv.at[slot], two_send_sem.at[slot], two_recv_sem.at[slot])
    features = (
        own_part[...]
        + two_recv[0].astype(F32)
        + two_recv[1].astype(F32)
        + two_recv[2].astype(F32)
    ).astype(BF16)
    _, slot_base = shift_of((dp_count * packed, slots), 1)
    packed_index = lax.broadcasted_iota(jnp.int32, (dp_count * packed, slots), 0)
    returned = jnp.zeros((dp_count * packed, LANES), F32)
    for n in range(groups):
        place = jnp.where(packed_index == slot_base + CAP * n, 1.0, 0.0).astype(BF16)
        returned = returned + dot(place, features[:, n * LANES : (n + 1) * LANES], NN)
    back_send[...] = returned.astype(BF16).reshape(dp_count, packed, LANES)
    back_recv[plane] = back_send[plane]
    for step in range(1, dp_count):
        other, device = at_plane(step)
        send(
            back_send.at[other],
            back_recv.at[plane],
            back_send_sem.at[step],
            back_recv_sem.at[plane],
            device,
        )

    for step in range(1, dp_count):
        other = (plane + step) % dp_count
        arrived(qz_recv.at[other], qz_send_sem.at[step], qz_recv_sem.at[other])
    q_rows = jnp.concatenate(
        [qz_recv[j, 0:1, :] for j in range(dp_count)] + [jnp.zeros((LANES - dp_count, LANES), F32)],
        axis=0,
    )
    q_columns = q_rows.T
    wanted = lax.broadcasted_iota(jnp.int32, (LANES, rows), 0).astype(F32) - (CAP * plane).astype(F32)
    found = [jnp.zeros((1, rows), F32), jnp.zeros((1, rows), F32)]
    for j, owner in enumerate(owners):
        hit = (wanted == jnp.broadcast_to(rank[j : j + 1, :], wanted.shape)) & (wanted >= 0.0)
        column = jnp.broadcast_to(q_columns[:, j : j + 1], wanted.shape)
        value = jnp.sum(jnp.where(hit, column, 0.0), axis=0, keepdims=True)
        for k in range(2):
            found[k] = found[k] + jnp.where(routes_ref[k : k + 1, :] == owner, value, 0.0)
    grad_probs_ref[...] = jnp.concatenate(found, axis=0)

    for step in range(1, dp_count):
        other = (plane + step) % dp_count
        arrived(back_recv.at[other], back_send_sem.at[step], back_recv_sem.at[other])
    stacked = dot(select, back_recv[...].reshape(dp_count * packed, LANES), TN)
    for n in range(groups):
        grad_tokens_ref[:, n * LANES : (n + 1) * LANES] = stacked[n * rows : (n + 1) * rows, :].astype(
            BF16
        )

    for copy in pending:
        copy.wait_send()
    x_copy.wait()
    d_copy.wait()


def outer_kernel(d_ref, x_ref, gate_ref, up_ref):
    width = x_ref.shape[2]
    for which, out in enumerate((gate_ref, up_ref)):
        left = d_ref[which]
        for index in range(x_ref.shape[0]):
            out[:, index * width : (index + 1) * width] = dot(left, x_ref[index], TN).astype(BF16)


def fused_body(dp_count, tokens, grad_out, routes, probs, gate_weight, up_weight, down_weight):
    rows, width = tokens.shape
    units, model = gate_weight.shape
    hidden_count = model // width
    groups = width // LANES
    packed = CAP * groups
    slots = CAP * dp_count
    large_count = dp_count // 6
    owners = tuple(j // 4 if j < 4 * large_count else j - 3 * large_count for j in range(dp_count))
    dma = pltpu.SemaphoreType.DMA
    vmem = pl.BlockSpec(memory_space=pltpu.VMEM)
    anywhere = pl.BlockSpec(memory_space=pl.ANY)
    grad_tokens, grad_probs, x_all, d_all = pl.pallas_call(
        functools.partial(fused_kernel, dp_count, owners),
        out_shape=(
            jax.ShapeDtypeStruct((rows, width), BF16),
            jax.ShapeDtypeStruct((2, rows), F32),
            jax.ShapeDtypeStruct((hidden_count, slots, width), BF16),
            jax.ShapeDtypeStruct((2, slots, units), BF16),
        ),
        in_specs=[vmem] * 4 + [anywhere] * 3,
        out_specs=(vmem, vmem, anywhere, anywhere),
        scratch_shapes=[
            pltpu.VMEM((3, hidden_count, units, width), BF16),
            dma((3, hidden_count)),
            pltpu.VMEM((2, hidden_count, slots, width), BF16),
            dma((2, 7)),
            dma((2, hidden_count)),
            pltpu.VMEM((2, dp_count, packed, LANES), BF16),
            pltpu.VMEM((2, dp_count, packed, LANES), BF16),
            dma((2, dp_count)),
            dma((2, dp_count)),
            pltpu.VMEM((dp_count, 8, LANES), F32),
            pltpu.VMEM((dp_count, 8, LANES), F32),
            dma((dp_count,)),
            dma((dp_count,)),
            pltpu.VMEM((3, slots, units), F32),
            pltpu.VMEM((2, slots, units), BF16),
            pltpu.VMEM((4, slots, width), BF16),
            pltpu.VMEM((4, slots, width), BF16),
            dma((4,)),
            dma((4,)),
            pltpu.VMEM((3, slots, width), BF16),
            pltpu.VMEM((3, slots, width), BF16),
            dma((3,)),
            dma((3,)),
            pltpu.VMEM((slots, width), F32),
            pltpu.VMEM((2, 8, LANES), F32),
            pltpu.VMEM((4, 8, LANES), F32),
            dma((4,)),
            dma((4,)),
            pltpu.VMEM((dp_count, packed, LANES), BF16),
            pltpu.VMEM((dp_count, packed, LANES), BF16),
            dma((dp_count,)),
            dma((dp_count,)),
            pltpu.VMEM((8, LANES), F32),
            pltpu.VMEM((dp_count, 8, LANES), F32),
            dma((dp_count,)),
            dma((dp_count,)),
            dma((2,)),
        ],
        compiler_params=pltpu.CompilerParams(
            collective_id=0, has_side_effects=True, vmem_limit_bytes=48 << 20
        ),
    )(routes.T, probs.T, tokens, grad_out, gate_weight, up_weight, down_weight)
    tile = LANES
    grad_gate, grad_up = pl.pallas_call(
        outer_kernel,
        grid=(units // tile,),
        out_shape=(jax.ShapeDtypeStruct((units, model), BF16),) * 2,
        in_specs=[
            pl.BlockSpec((2, slots, tile), lambda i: (0, 0, i)),
            pl.BlockSpec((hidden_count, slots, width), lambda i: (0, 0, 0)),
        ],
        out_specs=(pl.BlockSpec((tile, model), lambda i: (i, 0)),) * 2,
        compiler_params=pltpu.CompilerParams(vmem_limit_bytes=32 << 20),
    )(d_all, x_all)
    return (grad_tokens, grad_probs.T, grad_gate, grad_up)


def solution(mesh):
    placed = (
        P("dp", "hidden"),
        P("dp", "hidden"),
        P("dp", None),
        P("dp", None),
        P(("dp", "hidden"), None),
        P(("dp", "hidden"), None),
        P(("dp", "hidden"), None),
    )

    def local(tokens, grad_out, routes, probs, gate_weight, up_weight, down_weight):
        args = (tokens, grad_out, routes, probs, gate_weight, up_weight, down_weight)
        if fits(mesh.shape["dp"], mesh.shape["hidden"], tokens.shape, gate_weight.shape):
            return fused_body(mesh.shape["dp"], *args)
        return body(*args)

    return jax.shard_map(
        local,
        mesh=mesh,
        in_specs=placed,
        out_specs=(
            P("dp", "hidden"),
            P("dp", None),
            P(("dp", "hidden"), None),
            P(("dp", "hidden"), None),
        ),
        check_vma=False,
    )
```

```python
import functools

import jax
import jax.numpy as jnp
from jax import lax
from jax.experimental import pallas as pl
from jax.experimental.pallas import tpu as pltpu
from jax.sharding import PartitionSpec as P

CAP = 20


def body(tokens, grad_out, routes, probs, gate_weight, up_weight, down_weight):
    dp_count = lax.axis_size("dp")
    hidden_count = lax.axis_size("hidden")
    large_count = dp_count // 6
    expert_total = dp_count - 3 * large_count
    block_ids = jnp.arange(dp_count, dtype=jnp.int32)
    owners = jnp.where(block_ids < 4 * large_count, block_ids // 4, block_ids - 3 * large_count)
    expert_hits = (
        routes[:, :, None] == jnp.arange(expert_total, dtype=jnp.int32)[None, None, :]
    ).astype(jnp.int32)
    per_token = jnp.sum(expert_hits, axis=1)
    before = jnp.cumsum(per_token, axis=0) - per_token
    slot_rank = jnp.sum(expert_hits * before[:, None, :], axis=2)
    matches = routes[:, :, None] == owners[None, None, :]
    slot_hits = slot_rank[:, :, None, None] == jnp.arange(CAP, dtype=jnp.int32)[None, None, None, :]
    picked = (matches[:, :, :, None] & slot_hits).astype(jnp.float32)
    select = jnp.sum(picked, axis=1)
    select_half = select.astype(jnp.bfloat16)
    send_tokens = jnp.einsum(
        "tjc,td->jcd", select_half, tokens, preferred_element_type=jnp.float32
    ).astype(jnp.bfloat16)
    send_grads = jnp.einsum(
        "tjc,td->jcd", select_half, grad_out, preferred_element_type=jnp.float32
    ).astype(jnp.bfloat16)
    send_probs = jnp.einsum(
        "tkjc,tk->jc", picked, probs.astype(jnp.float32), precision=lax.Precision.HIGHEST
    ).astype(jnp.bfloat16)
    recv_tokens, recv_grads, recv_probs = (
        lax.all_to_all(send_tokens, "dp", split_axis=0, concat_axis=0, tiled=True),
        lax.all_to_all(send_grads, "dp", split_axis=0, concat_axis=0, tiled=True),
        lax.all_to_all(send_probs, "dp", split_axis=0, concat_axis=0, tiled=True),
    )
    row_count = dp_count * CAP
    contract = (((1,), (1,)), ((), ()))
    full_tokens, full_grads = (
        lax.all_gather(recv_tokens, "hidden", axis=2, tiled=True),
        lax.all_gather(recv_grads, "hidden", axis=2, tiled=True),
    )
    token_rows = full_tokens.reshape(row_count, full_tokens.shape[2])
    grad_rows = full_grads.reshape(row_count, full_grads.shape[2])
    back_pre = lax.dot_general(grad_rows, down_weight, contract, preferred_element_type=jnp.float32)
    slot_probs = recv_probs.reshape(row_count).astype(jnp.float32)
    gate_pre = lax.dot_general(
        token_rows, gate_weight, contract, preferred_element_type=jnp.float32
    )
    up_pre = lax.dot_general(token_rows, up_weight, contract, preferred_element_type=jnp.float32)
    sigmoid_gate = jax.nn.sigmoid(gate_pre)
    silu_gate = gate_pre * sigmoid_gate
    router_part = jnp.sum(silu_gate * up_pre * back_pre, axis=1)
    scaled = slot_probs[:, None] * back_pre
    grad_gate_pre = (
        scaled * up_pre * sigmoid_gate * (1.0 + gate_pre * (1.0 - sigmoid_gate))
    ).astype(jnp.bfloat16)
    grad_up_pre = (scaled * silu_gate).astype(jnp.bfloat16)
    over_rows = (((0,), (0,)), ((), ()))
    grad_gate = lax.dot_general(
        grad_gate_pre, token_rows, over_rows, preferred_element_type=jnp.float32
    ).astype(jnp.bfloat16)
    grad_up = lax.dot_general(
        grad_up_pre, token_rows, over_rows, preferred_element_type=jnp.float32
    ).astype(jnp.bfloat16)
    feature_width = gate_weight.shape[1] // hidden_count
    cross = (((0,), (1,)), ((), ()))
    own_features = lax.psum_scatter(
        lax.dot_general(gate_weight, grad_gate_pre, cross, preferred_element_type=jnp.float32)
        + lax.dot_general(up_weight, grad_up_pre, cross, preferred_element_type=jnp.float32),
        "hidden",
        scatter_dimension=0,
        tiled=True,
    ).T
    router_payload = lax.psum(router_part, "hidden")
    back_features, back_router = (
        lax.all_to_all(
            own_features.reshape(dp_count, CAP, feature_width),
            "dp",
            split_axis=0,
            concat_axis=0,
            tiled=True,
        ),
        lax.all_to_all(
            router_payload.reshape(dp_count, CAP), "dp", split_axis=0, concat_axis=0, tiled=True
        ),
    )
    token_router = jnp.einsum("tkjc,jc->tk", picked, back_router, precision=lax.Precision.HIGHEST)
    grad_tokens = jnp.einsum(
        "tjc,jcd->td", select, back_features, precision=lax.Precision.HIGHEST
    ).astype(jnp.bfloat16)
    return (grad_tokens, token_router, grad_gate, grad_up)


LANES = 128
MESH = pl.DeviceIdType.MESH
F32 = jnp.float32
BF16 = jnp.bfloat16
NT = (((1,), (1,)), ((), ()))
NN = (((1,), (0,)), ((), ()))
TN = (((0,), (0,)), ((), ()))


def fits(dp_count, hidden_count, token_shape, weight_shape):
    rows, width = token_shape
    groups = width // LANES
    return (
        hidden_count == 8
        and 2 <= dp_count <= 8
        and width % LANES == 0
        and rows * groups == LANES
        and (CAP * groups) % 16 == 0
        and (CAP * dp_count) % 16 == 0
        and CAP * dp_count <= LANES
        and weight_shape[0] % LANES == 0
    )


def dot(a, b, dims):
    return lax.dot_general(a, b, dims, preferred_element_type=F32)


def steps_of(values, size, count):
    total = jnp.zeros_like(values)
    for edge in range(1, count):
        total = total + (values >= edge * size).astype(jnp.int32)
    return total


def fused_kernel(
    dp_count,
    owners,
    routes_hbm,
    probs_hbm,
    tokens_hbm,
    grads_hbm,
    gate_hbm,
    up_hbm,
    down_hbm,
    grad_tokens_ref,
    grad_probs_ref,
    x_out,
    d_out,
    weights,
    weight_sem,
    xbuf,
    x_send,
    x_recv,
    zsend,
    zrecv,
    z_send_sem,
    z_recv_sem,
    aux_send,
    aux_recv,
    aux_send_sem,
    aux_recv_sem,
    acc,
    tbuf,
    dbuf,
    one_send,
    one_recv,
    one_send_sem,
    one_recv_sem,
    two_send,
    two_recv,
    two_send_sem,
    two_recv_sem,
    own_part,
    q_send,
    q_recv,
    q_send_sem,
    q_recv_sem,
    back_send,
    back_recv,
    back_send_sem,
    back_recv_sem,
    qz_send,
    qz_recv,
    qz_send_sem,
    qz_recv_sem,
    out_sem,
    routes_ref,
    probs_ref,
    tokens_ref,
    grads_ref,
    in_sem,
):
    rows, width = tokens_ref.shape
    groups = width // LANES
    packed = CAP * groups
    slots = CAP * dp_count
    plane = lax.axis_index("dp")
    h = lax.axis_index("hidden")
    core = h % 2
    x_pos = (h // 2) % 2
    y_pos = h // 4
    to_sib = 1 - 2 * core
    sib = h + to_sib
    hx = h + 2 - 4 * x_pos
    hy = h + 4 - 8 * y_pos
    hd = hx + 4 - 8 * y_pos

    def at_hidden(index):
        return (plane, index)

    def at_plane(step):
        other = (plane + step) % dp_count
        return other, (other, h)

    inputs = [
        pltpu.make_async_copy(source, target, in_sem.at[n])
        for n, (source, target) in enumerate(
            (
                (routes_hbm, routes_ref),
                (probs_hbm, probs_ref),
                (tokens_hbm, tokens_ref),
                (grads_hbm, grads_ref),
            )
        )
    ]
    for copy in inputs:
        copy.start()

    barrier = pltpu.get_barrier_semaphore()
    for index in (sib, hx, hy, hd):
        pl.semaphore_signal(barrier, inc=1, device_id=at_hidden(index), device_id_type=MESH)
    for step in range(1, dp_count):
        pl.semaphore_signal(barrier, inc=1, device_id=at_plane(step)[1], device_id_type=MESH)

    order = (h, sib, hx, hy, hx + to_sib, hy + to_sib, hd, hd + to_sib)

    def weight_copy(which, index):
        columns = pl.ds(pl.multiple_of(index * width, width), width)
        source = (gate_hbm, up_hbm, down_hbm)[which]
        return pltpu.make_async_copy(
            source.at[:, columns], weights.at[which, index], weight_sem.at[which, index]
        )

    def fetch_weights(indices):
        for index in indices:
            for which in range(3):
                weight_copy(which, index).start()

    pending = []

    def send(source, target, send_sem, recv_sem, device):
        copy = pltpu.make_async_remote_copy(
            src_ref=source,
            dst_ref=target,
            send_sem=send_sem,
            recv_sem=recv_sem,
            device_id=device,
            device_id_type=MESH,
        )
        copy.start()
        pending.append(copy)

    def arrived(target, send_sem, recv_sem):
        pltpu.make_async_remote_copy(
            src_ref=target,
            dst_ref=target,
            send_sem=send_sem,
            recv_sem=recv_sem,
            device_id=at_hidden(sib),
            device_id_type=MESH,
        ).wait_recv()

    block_row = lax.broadcasted_iota(jnp.int32, (8, rows), 0)
    owner_of = jnp.full((8, rows), -1, jnp.int32)
    for j, owner in enumerate(owners):
        owner_of = jnp.where(block_row == j, owner, owner_of)
    inputs[0].wait()
    inputs[1].wait()
    first = jnp.broadcast_to(routes_ref[0:1, :], (8, rows))
    second = jnp.broadcast_to(routes_ref[1:2, :], (8, rows))
    prob_rows = probs_ref[...].astype(F32)
    match = (owner_of == first) | (owner_of == second)
    earlier = lax.broadcasted_iota(jnp.int32, (rows, rows), 0) < lax.broadcasted_iota(
        jnp.int32, (rows, rows), 1
    )
    rank = dot(match.astype(F32).astype(BF16), earlier.astype(F32).astype(BF16), NN)
    rank = jnp.where(match, rank, -1.0)
    block_prob = jnp.where(owner_of == first, jnp.broadcast_to(prob_rows[0:1, :], (8, rows)), 0.0)
    block_prob = block_prob + jnp.where(
        owner_of == second, jnp.broadcast_to(prob_rows[1:2, :], (8, rows)), 0.0
    )
    for j in range(dp_count):
        aux_send[j] = jnp.zeros((8, LANES), F32)
        aux_send[j, 0:1, 0:rows] = rank[j : j + 1, :]
        aux_send[j, 1:2, 0:rows] = block_prob[j : j + 1, :]
    wide_rank = jnp.concatenate([rank] * groups, axis=1)
    pack_row = lax.broadcasted_iota(jnp.int32, (packed, LANES), 0)
    pack_group = steps_of(pack_row, CAP, groups)
    pack_slot = (pack_row - CAP * pack_group).astype(F32)
    lane_group = steps_of(lax.broadcasted_iota(jnp.int32, (packed, LANES), 1), rows, groups)
    same_group = pack_group == lane_group
    select = jnp.concatenate(
        [
            jnp.where(
                same_group & (pack_slot == jnp.broadcast_to(wide_rank[j : j + 1, :], pack_slot.shape)),
                1.0,
                0.0,
            )
            for j in range(dp_count)
        ],
        axis=0,
    ).astype(BF16)

    for a, ref in enumerate((tokens_ref, grads_ref)):
        inputs[2 + a].wait()
        stacked = jnp.concatenate(
            [ref[:, n * LANES : (n + 1) * LANES] for n in range(groups)], axis=0
        )
        zsend[a] = dot(select, stacked, NN).astype(BF16).reshape(dp_count, packed, LANES)
        zrecv[a, plane] = zsend[a, plane]
        if a == 0:
            aux_recv[plane] = aux_send[plane]
            pl.semaphore_wait(barrier, 4 + dp_count - 1)
        for step in range(1, dp_count):
            other, device = at_plane(step)
            send(
                zsend.at[a, other],
                zrecv.at[a, plane],
                z_send_sem.at[a, step],
                z_recv_sem.at[a, plane],
                device,
            )
    for step in range(1, dp_count):
        other, device = at_plane(step)
        send(
            aux_send.at[other],
            aux_recv.at[plane],
            aux_send_sem.at[step],
            aux_recv_sem.at[plane],
            device,
        )

    fetch_weights(order[:4])

    def shift_of(shape, axis):
        slot = lax.broadcasted_iota(jnp.int32, shape, axis)
        return slot, slot + (packed - CAP) * steps_of(slot, CAP, dp_count)

    slot_index, slot_base = shift_of((slots, dp_count * packed), 0)
    packed_index = lax.broadcasted_iota(jnp.int32, (slots, dp_count * packed), 1)
    unpack = [
        jnp.where(packed_index == slot_base + CAP * n, 1.0, 0.0).astype(BF16) for n in range(groups)
    ]
    for a in range(2):
        for step in range(1, dp_count):
            other = (plane + step) % dp_count
            arrived(zrecv.at[a, other], z_send_sem.at[a, step], z_recv_sem.at[a, other])
        received = zrecv[a].reshape(dp_count * packed, LANES)
        for n in range(groups):
            xbuf[a, h, :, n * LANES : (n + 1) * LANES] = dot(unpack[n], received, NN).astype(BF16)
        for slot, partner in enumerate((hx, hy, sib)):
            send(
                xbuf.at[a, h],
                xbuf.at[a, h],
                x_send.at[a, slot],
                x_recv.at[a, h],
                at_hidden(partner),
            )

    fetch_weights(order[4:6])

    def wait_x(a, index):
        arrived(xbuf.at[a, index], x_send.at[a, 0], x_recv.at[a, index])

    def forward(a, index, partner, slot):
        send(
            xbuf.at[a, index],
            xbuf.at[a, index],
            x_send.at[a, slot],
            x_recv.at[a, index],
            at_hidden(partner),
        )

    def project(which, index, start):
        weight_copy(which, index).wait()
        part = dot(weights[which, index], xbuf[0 if which < 2 else 1, index], NT)
        acc[which] = part if start else acc[which] + part

    def project_all(index):
        for which in range(3):
            project(which, index, False)

    project(0, h, True)
    project(1, h, True)
    wait_x(0, hx)
    forward(0, hx, hy, 3)
    forward(0, hx, sib, 4)
    wait_x(0, hy)
    forward(0, hy, sib, 5)
    project(2, h, True)
    wait_x(1, hy)
    forward(1, hy, hx, 3)
    forward(1, hy, sib, 4)
    wait_x(1, hx)
    forward(1, hx, sib, 5)
    fetch_weights(order[6:])
    wait_x(0, sib)
    wait_x(1, sib)
    project_all(sib)
    project_all(hx)
    wait_x(0, hd)
    forward(0, hd, sib, 6)
    wait_x(1, hd)
    forward(1, hd, sib, 6)
    project_all(hy)
    for index in (hx + to_sib, hy + to_sib):
        wait_x(0, index)
        wait_x(1, index)
        project_all(index)
    project_all(hd)
    wait_x(0, hd + to_sib)
    wait_x(1, hd + to_sib)
    project_all(hd + to_sib)
    x_copy = pltpu.make_async_copy(xbuf.at[0], x_out, out_sem.at[0])
    x_copy.start()

    for step in range(1, dp_count):
        other = (plane + step) % dp_count
        arrived(aux_recv.at[other], aux_send_sem.at[step], aux_recv_sem.at[other])
    slot_value = lax.broadcasted_iota(jnp.int32, (slots, rows), 0).astype(F32)
    slot_prob = jnp.zeros((slots, 1), F32)
    for source in range(dp_count):
        source_rank = jnp.broadcast_to(aux_recv[source, 0:1, 0:rows], (slots, rows))
        source_prob = jnp.broadcast_to(aux_recv[source, 1:2, 0:rows], (slots, rows))
        hit = (source_rank >= 0.0) & (slot_value == source_rank + float(CAP * source))
        slot_prob = slot_prob + jnp.sum(jnp.where(hit, source_prob, 0.0), axis=1, keepdims=True)

    def tall(values, count):
        gap = jnp.zeros((LANES - count, values.shape[1]), F32)
        return jnp.concatenate([values, gap], axis=0) if count < LANES else values

    prob_row = tall(jnp.broadcast_to(slot_prob, (slots, LANES)), slots).T[0:1, 0:slots]
    gate_pre = acc[0]
    up_pre = acc[1]
    back_pre = acc[2]
    sigmoid_gate = jax.nn.sigmoid(gate_pre)
    silu_gate = gate_pre * sigmoid_gate
    scaled = prob_row * back_pre
    grad_gate_pre = scaled * up_pre * sigmoid_gate * (1.0 + gate_pre * (1.0 - sigmoid_gate))
    grad_up_pre = scaled * silu_gate
    for which, value in enumerate((grad_gate_pre, grad_up_pre)):
        tbuf[which] = value.astype(BF16)
        dbuf[which] = value.T.astype(BF16)
    router = jnp.sum(silu_gate * up_pre * back_pre, axis=0, keepdims=True)
    d_copy = pltpu.make_async_copy(tbuf, d_out, out_sem.at[1])
    d_copy.start()
    q_send[0] = jnp.zeros((8, LANES), F32)
    q_send[0, 0:1, 0:slots] = router
    send(q_send.at[0], q_recv.at[0], q_send_sem.at[0], q_recv_sem.at[0], at_hidden(sib))

    def partial(index):
        return dot(dbuf[0], weights[0, index], NN) + dot(dbuf[1], weights[1, index], NN)

    chips = (hd, hx, hy, h)

    def sibling_part(slot):
        one_send[slot] = partial(chips[slot] + to_sib).astype(BF16)
        send(
            one_send.at[slot],
            one_recv.at[slot],
            one_send_sem.at[slot],
            one_recv_sem.at[slot],
            at_hidden(sib),
        )

    sibling_part(0)
    arrived(q_recv.at[0], q_send_sem.at[0], q_recv_sem.at[0])
    q_send[1] = q_send[0] + q_recv[0]
    for slot, index in enumerate((hd, hx, hy)):
        send(
            q_send.at[1],
            q_recv.at[1 + slot],
            q_send_sem.at[1 + slot],
            q_recv_sem.at[1 + slot],
            at_hidden(index),
        )
    for slot, index in enumerate(chips):
        if slot < 3:
            sibling_part(slot + 1)
        own = partial(index)
        arrived(one_recv.at[slot], one_send_sem.at[slot], one_recv_sem.at[slot])
        total = own + one_recv[slot].astype(F32)
        if slot == 3:
            own_part[...] = total
        else:
            two_send[slot] = total.astype(BF16)
            send(
                two_send.at[slot],
                two_recv.at[slot],
                two_send_sem.at[slot],
                two_recv_sem.at[slot],
                at_hidden(index),
            )

    for slot in range(3):
        arrived(q_recv.at[1 + slot], q_send_sem.at[1 + slot], q_recv_sem.at[1 + slot])
    q_total = (q_send[1] + q_recv[2]) + (q_recv[3] + q_recv[1])
    qz_send[...] = q_total
    qz_recv[plane] = q_total
    for step in range(1, dp_count):
        _, device = at_plane(step)
        send(qz_send, qz_recv.at[plane], qz_send_sem.at[step], qz_recv_sem.at[plane], device)

    for slot in range(3):
        arrived(two_recv.at[slot], two_send_sem.at[slot], two_recv_sem.at[slot])
    features = (
        own_part[...]
        + two_recv[0].astype(F32)
        + two_recv[1].astype(F32)
        + two_recv[2].astype(F32)
    ).astype(BF16)
    _, slot_base = shift_of((dp_count * packed, slots), 1)
    packed_index = lax.broadcasted_iota(jnp.int32, (dp_count * packed, slots), 0)
    returned = jnp.zeros((dp_count * packed, LANES), F32)
    for n in range(groups):
        place = jnp.where(packed_index == slot_base + CAP * n, 1.0, 0.0).astype(BF16)
        returned = returned + dot(place, features[:, n * LANES : (n + 1) * LANES], NN)
    back_send[...] = returned.astype(BF16).reshape(dp_count, packed, LANES)
    back_recv[plane] = back_send[plane]
    for step in range(1, dp_count):
        other, device = at_plane(step)
        send(
            back_send.at[other],
            back_recv.at[plane],
            back_send_sem.at[step],
            back_recv_sem.at[plane],
            device,
        )

    for step in range(1, dp_count):
        other = (plane + step) % dp_count
        arrived(qz_recv.at[other], qz_send_sem.at[step], qz_recv_sem.at[other])
    q_rows = jnp.concatenate(
        [qz_recv[j, 0:1, :] for j in range(dp_count)] + [jnp.zeros((LANES - dp_count, LANES), F32)],
        axis=0,
    )
    q_columns = q_rows.T
    wanted = lax.broadcasted_iota(jnp.int32, (LANES, rows), 0).astype(F32) - (CAP * plane).astype(F32)
    found = [jnp.zeros((1, rows), F32), jnp.zeros((1, rows), F32)]
    for j, owner in enumerate(owners):
        hit = (wanted == jnp.broadcast_to(rank[j : j + 1, :], wanted.shape)) & (wanted >= 0.0)
        column = jnp.broadcast_to(q_columns[:, j : j + 1], wanted.shape)
        value = jnp.sum(jnp.where(hit, column, 0.0), axis=0, keepdims=True)
        for k in range(2):
            found[k] = found[k] + jnp.where(routes_ref[k : k + 1, :] == owner, value, 0.0)
    grad_probs_ref[...] = jnp.concatenate(found, axis=0)

    for step in range(1, dp_count):
        other = (plane + step) % dp_count
        arrived(back_recv.at[other], back_send_sem.at[step], back_recv_sem.at[other])
    stacked = dot(select, back_recv[...].reshape(dp_count * packed, LANES), TN)
    for n in range(groups):
        grad_tokens_ref[:, n * LANES : (n + 1) * LANES] = stacked[n * rows : (n + 1) * rows, :].astype(
            BF16
        )

    for copy in pending:
        copy.wait_send()
    x_copy.wait()
    d_copy.wait()


def outer_kernel(d_ref, x_ref, tokens_ref, probs_ref, gate_ref, up_ref, tokens_out, probs_out):
    gate_ref[...] = dot(d_ref[0], x_ref[0], NN).astype(BF16)
    up_ref[...] = dot(d_ref[1], x_ref[0], NN).astype(BF16)

    @pl.when(pl.program_id(0) == 0)
    def _():
        tokens_out[...] = tokens_ref[...]
        probs_out[...] = probs_ref[...]


def fused_body(dp_count, tokens, grad_out, routes, probs, gate_weight, up_weight, down_weight):
    rows, width = tokens.shape
    units, model = gate_weight.shape
    hidden_count = model // width
    groups = width // LANES
    packed = CAP * groups
    slots = CAP * dp_count
    large_count = dp_count // 6
    owners = tuple(j // 4 if j < 4 * large_count else j - 3 * large_count for j in range(dp_count))
    dma = pltpu.SemaphoreType.DMA
    vmem = pl.BlockSpec(memory_space=pltpu.VMEM)
    anywhere = pl.BlockSpec(memory_space=pl.ANY)
    grad_tokens, grad_probs, x_all, d_all = pl.pallas_call(
        functools.partial(fused_kernel, dp_count, owners),
        out_shape=(
            jax.ShapeDtypeStruct((rows, width), BF16),
            jax.ShapeDtypeStruct((2, rows), F32),
            jax.ShapeDtypeStruct((hidden_count, slots, width), BF16),
            jax.ShapeDtypeStruct((2, units, slots), BF16),
        ),
        in_specs=[pl.BlockSpec(memory_space=pltpu.HBM)] * 7,
        out_specs=(vmem, vmem, anywhere, anywhere),
        scratch_shapes=[
            pltpu.VMEM((3, hidden_count, units, width), BF16),
            dma((3, hidden_count)),
            pltpu.VMEM((2, hidden_count, slots, width), BF16),
            dma((2, 7)),
            dma((2, hidden_count)),
            pltpu.VMEM((2, dp_count, packed, LANES), BF16),
            pltpu.VMEM((2, dp_count, packed, LANES), BF16),
            dma((2, dp_count)),
            dma((2, dp_count)),
            pltpu.VMEM((dp_count, 8, LANES), F32),
            pltpu.VMEM((dp_count, 8, LANES), F32),
            dma((dp_count,)),
            dma((dp_count,)),
            pltpu.VMEM((3, units, slots), F32),
            pltpu.VMEM((2, units, slots), BF16),
            pltpu.VMEM((2, slots, units), BF16),
            pltpu.VMEM((4, slots, width), BF16),
            pltpu.VMEM((4, slots, width), BF16),
            dma((4,)),
            dma((4,)),
            pltpu.VMEM((3, slots, width), BF16),
            pltpu.VMEM((3, slots, width), BF16),
            dma((3,)),
            dma((3,)),
            pltpu.VMEM((slots, width), F32),
            pltpu.VMEM((2, 8, LANES), F32),
            pltpu.VMEM((4, 8, LANES), F32),
            dma((4,)),
            dma((4,)),
            pltpu.VMEM((dp_count, packed, LANES), BF16),
            pltpu.VMEM((dp_count, packed, LANES), BF16),
            dma((dp_count,)),
            dma((dp_count,)),
            pltpu.VMEM((8, LANES), F32),
            pltpu.VMEM((dp_count, 8, LANES), F32),
            dma((dp_count,)),
            dma((dp_count,)),
            dma((2,)),
            pltpu.VMEM((2, rows), jnp.int32),
            pltpu.VMEM((2, rows), BF16),
            pltpu.VMEM((rows, width), BF16),
            pltpu.VMEM((rows, width), BF16),
            dma((4,)),
        ],
        compiler_params=pltpu.CompilerParams(
            collective_id=0, has_side_effects=True, vmem_limit_bytes=64 << 20
        ),
    )(routes.T, probs.T, tokens, grad_out, gate_weight, up_weight, down_weight)
    grad_gate, grad_up, grad_tokens, grad_probs = pl.pallas_call(
        outer_kernel,
        grid=(hidden_count,),
        out_shape=(
            jax.ShapeDtypeStruct((units, model), BF16),
            jax.ShapeDtypeStruct((units, model), BF16),
            jax.ShapeDtypeStruct((rows, width), BF16),
            jax.ShapeDtypeStruct((2, rows), F32),
        ),
        in_specs=[
            pl.BlockSpec((2, units, slots), lambda i: (0, 0, 0)),
            pl.BlockSpec((1, slots, width), lambda i: (i, 0, 0)),
            pl.BlockSpec((rows, width), lambda i: (0, 0)),
            pl.BlockSpec((2, rows), lambda i: (0, 0)),
        ],
        out_specs=(
            pl.BlockSpec((units, width), lambda i: (0, i)),
            pl.BlockSpec((units, width), lambda i: (0, i)),
            pl.BlockSpec((rows, width), lambda i: (0, 0)),
            pl.BlockSpec((2, rows), lambda i: (0, 0)),
        ),
        compiler_params=pltpu.CompilerParams(vmem_limit_bytes=64 << 20),
    )(d_all, x_all, grad_tokens, grad_probs)
    return (grad_tokens, grad_probs.T, grad_gate, grad_up)


def solution(mesh):
    placed = (
        P("dp", "hidden"),
        P("dp", "hidden"),
        P("dp", None),
        P("dp", None),
        P(("dp", "hidden"), None),
        P(("dp", "hidden"), None),
        P(("dp", "hidden"), None),
    )

    def local(tokens, grad_out, routes, probs, gate_weight, up_weight, down_weight):
        args = (tokens, grad_out, routes, probs, gate_weight, up_weight, down_weight)
        if fits(mesh.shape["dp"], mesh.shape["hidden"], tokens.shape, gate_weight.shape):
            return fused_body(mesh.shape["dp"], *args)
        return body(*args)

    return jax.shard_map(
        local,
        mesh=mesh,
        in_specs=placed,
        out_specs=(
            P("dp", "hidden"),
            P("dp", None),
            P(("dp", "hidden"), None),
            P(("dp", "hidden"), None),
        ),
        check_vma=False,
    )
```

```python
import functools

import jax
import jax.numpy as jnp
from jax import lax
from jax.experimental import pallas as pl
from jax.experimental.pallas import tpu as pltpu
from jax.sharding import PartitionSpec as P

CAP = 20


def body(tokens, grad_out, routes, probs, gate_weight, up_weight, down_weight):
    dp_count = lax.axis_size("dp")
    hidden_count = lax.axis_size("hidden")
    large_count = dp_count // 6
    expert_total = dp_count - 3 * large_count
    block_ids = jnp.arange(dp_count, dtype=jnp.int32)
    owners = jnp.where(block_ids < 4 * large_count, block_ids // 4, block_ids - 3 * large_count)
    expert_hits = (
        routes[:, :, None] == jnp.arange(expert_total, dtype=jnp.int32)[None, None, :]
    ).astype(jnp.int32)
    per_token = jnp.sum(expert_hits, axis=1)
    before = jnp.cumsum(per_token, axis=0) - per_token
    slot_rank = jnp.sum(expert_hits * before[:, None, :], axis=2)
    matches = routes[:, :, None] == owners[None, None, :]
    slot_hits = slot_rank[:, :, None, None] == jnp.arange(CAP, dtype=jnp.int32)[None, None, None, :]
    picked = (matches[:, :, :, None] & slot_hits).astype(jnp.float32)
    select = jnp.sum(picked, axis=1)
    select_half = select.astype(jnp.bfloat16)
    send_tokens = jnp.einsum(
        "tjc,td->jcd", select_half, tokens, preferred_element_type=jnp.float32
    ).astype(jnp.bfloat16)
    send_grads = jnp.einsum(
        "tjc,td->jcd", select_half, grad_out, preferred_element_type=jnp.float32
    ).astype(jnp.bfloat16)
    send_probs = jnp.einsum(
        "tkjc,tk->jc", picked, probs.astype(jnp.float32), precision=lax.Precision.HIGHEST
    ).astype(jnp.bfloat16)
    recv_tokens, recv_grads, recv_probs = (
        lax.all_to_all(send_tokens, "dp", split_axis=0, concat_axis=0, tiled=True),
        lax.all_to_all(send_grads, "dp", split_axis=0, concat_axis=0, tiled=True),
        lax.all_to_all(send_probs, "dp", split_axis=0, concat_axis=0, tiled=True),
    )
    row_count = dp_count * CAP
    contract = (((1,), (1,)), ((), ()))
    full_tokens, full_grads = (
        lax.all_gather(recv_tokens, "hidden", axis=2, tiled=True),
        lax.all_gather(recv_grads, "hidden", axis=2, tiled=True),
    )
    token_rows = full_tokens.reshape(row_count, full_tokens.shape[2])
    grad_rows = full_grads.reshape(row_count, full_grads.shape[2])
    back_pre = lax.dot_general(grad_rows, down_weight, contract, preferred_element_type=jnp.float32)
    slot_probs = recv_probs.reshape(row_count).astype(jnp.float32)
    gate_pre = lax.dot_general(
        token_rows, gate_weight, contract, preferred_element_type=jnp.float32
    )
    up_pre = lax.dot_general(token_rows, up_weight, contract, preferred_element_type=jnp.float32)
    sigmoid_gate = jax.nn.sigmoid(gate_pre)
    silu_gate = gate_pre * sigmoid_gate
    router_part = jnp.sum(silu_gate * up_pre * back_pre, axis=1)
    scaled = slot_probs[:, None] * back_pre
    grad_gate_pre = (
        scaled * up_pre * sigmoid_gate * (1.0 + gate_pre * (1.0 - sigmoid_gate))
    ).astype(jnp.bfloat16)
    grad_up_pre = (scaled * silu_gate).astype(jnp.bfloat16)
    over_rows = (((0,), (0,)), ((), ()))
    grad_gate = lax.dot_general(
        grad_gate_pre, token_rows, over_rows, preferred_element_type=jnp.float32
    ).astype(jnp.bfloat16)
    grad_up = lax.dot_general(
        grad_up_pre, token_rows, over_rows, preferred_element_type=jnp.float32
    ).astype(jnp.bfloat16)
    feature_width = gate_weight.shape[1] // hidden_count
    cross = (((0,), (1,)), ((), ()))
    own_features = lax.psum_scatter(
        lax.dot_general(gate_weight, grad_gate_pre, cross, preferred_element_type=jnp.float32)
        + lax.dot_general(up_weight, grad_up_pre, cross, preferred_element_type=jnp.float32),
        "hidden",
        scatter_dimension=0,
        tiled=True,
    ).T
    router_payload = lax.psum(router_part, "hidden")
    back_features, back_router = (
        lax.all_to_all(
            own_features.reshape(dp_count, CAP, feature_width),
            "dp",
            split_axis=0,
            concat_axis=0,
            tiled=True,
        ),
        lax.all_to_all(
            router_payload.reshape(dp_count, CAP), "dp", split_axis=0, concat_axis=0, tiled=True
        ),
    )
    token_router = jnp.einsum("tkjc,jc->tk", picked, back_router, precision=lax.Precision.HIGHEST)
    grad_tokens = jnp.einsum(
        "tjc,jcd->td", select, back_features, precision=lax.Precision.HIGHEST
    ).astype(jnp.bfloat16)
    return (grad_tokens, token_router, grad_gate, grad_up)


LANES = 128
MESH = pl.DeviceIdType.MESH
F32 = jnp.float32
BF16 = jnp.bfloat16
NT = (((1,), (1,)), ((), ()))
NN = (((1,), (0,)), ((), ()))
TN = (((0,), (0,)), ((), ()))


def fits(dp_count, hidden_count, token_shape, weight_shape):
    rows, width = token_shape
    groups = width // LANES
    return (
        hidden_count == 8
        and 2 <= dp_count <= 8
        and width % LANES == 0
        and rows * groups == LANES
        and (CAP * groups) % 16 == 0
        and (CAP * dp_count) % 16 == 0
        and CAP * dp_count <= LANES
        and weight_shape[0] % LANES == 0
    )


def dot(a, b, dims):
    return lax.dot_general(a, b, dims, preferred_element_type=F32)


def strips(total, size):
    return [(start, min(size, total - start)) for start in range(0, total, size)]


def steps_of(values, size, count):
    total = jnp.zeros_like(values)
    for edge in range(1, count):
        total = total + (values >= edge * size).astype(jnp.int32)
    return total


def fused_kernel(
    dp_count,
    owners,
    routes_hbm,
    probs_hbm,
    tokens_hbm,
    grads_hbm,
    gate_hbm,
    up_hbm,
    down_hbm,
    grad_tokens_ref,
    grad_probs_ref,
    x_out,
    d_out,
    weights,
    weight_sem,
    xbuf,
    x_send,
    x_recv,
    zsend,
    zrecv,
    z_send_sem,
    z_recv_sem,
    aux_send,
    aux_recv,
    aux_send_sem,
    aux_recv_sem,
    acc,
    dbuf,
    one_send,
    one_recv,
    one_send_sem,
    one_recv_sem,
    two_send,
    two_recv,
    two_send_sem,
    two_recv_sem,
    own_part,
    q_send,
    q_recv,
    q_send_sem,
    q_recv_sem,
    back_send,
    back_recv,
    back_send_sem,
    back_recv_sem,
    qz_send,
    qz_recv,
    qz_send_sem,
    qz_recv_sem,
    out_sem,
    routes_ref,
    probs_ref,
    tokens_ref,
    grads_ref,
    in_sem,
):
    rows, width = tokens_ref.shape
    units = gate_hbm.shape[0]
    groups = width // LANES
    packed = CAP * groups
    slots = CAP * dp_count
    plane = lax.axis_index("dp")
    h = lax.axis_index("hidden")
    core = h % 2
    x_pos = (h // 2) % 2
    y_pos = h // 4
    to_sib = 1 - 2 * core
    sib = h + to_sib
    hx = h + 2 - 4 * x_pos
    hy = h + 4 - 8 * y_pos
    hd = hx + 4 - 8 * y_pos

    def at_hidden(index):
        return (plane, index)

    def at_plane(step):
        other = (plane + step) % dp_count
        return other, (other, h)

    inputs = [
        pltpu.make_async_copy(source, target, in_sem.at[n])
        for n, (source, target) in enumerate(
            (
                (routes_hbm, routes_ref),
                (probs_hbm, probs_ref),
                (tokens_hbm, tokens_ref),
                (grads_hbm, grads_ref),
            )
        )
    ]
    for copy in inputs:
        copy.start()

    barrier = pltpu.get_barrier_semaphore()
    for index in (sib, hx, hy, hd):
        pl.semaphore_signal(barrier, inc=1, device_id=at_hidden(index), device_id_type=MESH)
    for step in range(1, dp_count):
        pl.semaphore_signal(barrier, inc=1, device_id=at_plane(step)[1], device_id_type=MESH)

    order = (h, sib, hx, hy, hx + to_sib, hy + to_sib, hd, hd + to_sib)

    def weight_copy(which, index):
        columns = pl.ds(pl.multiple_of(index * width, width), width)
        source = (gate_hbm, up_hbm, down_hbm)[which]
        return pltpu.make_async_copy(
            source.at[:, columns], weights.at[which, index], weight_sem.at[which, index]
        )

    def fetch_weights(indices):
        for index in indices:
            for which in range(3):
                weight_copy(which, index).start()

    fetch_weights(order[:2])
    pending = []

    def send(source, target, send_sem, recv_sem, device):
        copy = pltpu.make_async_remote_copy(
            src_ref=source,
            dst_ref=target,
            send_sem=send_sem,
            recv_sem=recv_sem,
            device_id=device,
            device_id_type=MESH,
        )
        copy.start()
        pending.append(copy)

    def arrived(target, send_sem, recv_sem):
        pltpu.make_async_remote_copy(
            src_ref=target,
            dst_ref=target,
            send_sem=send_sem,
            recv_sem=recv_sem,
            device_id=at_hidden(sib),
            device_id_type=MESH,
        ).wait_recv()

    block_row = lax.broadcasted_iota(jnp.int32, (8, rows), 0)
    owner_of = jnp.full((8, rows), -1, jnp.int32)
    for j, owner in enumerate(owners):
        owner_of = jnp.where(block_row == j, owner, owner_of)
    inputs[0].wait()
    inputs[1].wait()
    first = jnp.broadcast_to(routes_ref[0:1, :], (8, rows))
    second = jnp.broadcast_to(routes_ref[1:2, :], (8, rows))
    prob_rows = probs_ref[...].astype(F32)
    match = (owner_of == first) | (owner_of == second)
    earlier = lax.broadcasted_iota(jnp.int32, (rows, rows), 0) < lax.broadcasted_iota(
        jnp.int32, (rows, rows), 1
    )
    rank = dot(match.astype(F32).astype(BF16), earlier.astype(F32).astype(BF16), NN)
    rank = jnp.where(match, rank, -1.0)
    block_prob = jnp.where(owner_of == first, jnp.broadcast_to(prob_rows[0:1, :], (8, rows)), 0.0)
    block_prob = block_prob + jnp.where(
        owner_of == second, jnp.broadcast_to(prob_rows[1:2, :], (8, rows)), 0.0
    )
    for j in range(dp_count):
        aux_send[j] = jnp.zeros((8, LANES), F32)
        aux_send[j, 0:1, 0:rows] = rank[j : j + 1, :]
        aux_send[j, 1:2, 0:rows] = block_prob[j : j + 1, :]
    wide_rank = jnp.concatenate([rank] * groups, axis=1)
    pack_row = lax.broadcasted_iota(jnp.int32, (packed, LANES), 0)
    pack_group = steps_of(pack_row, CAP, groups)
    pack_slot = (pack_row - CAP * pack_group).astype(F32)
    lane_group = steps_of(lax.broadcasted_iota(jnp.int32, (packed, LANES), 1), rows, groups)
    same_group = pack_group == lane_group
    select = jnp.concatenate(
        [
            jnp.where(
                same_group & (pack_slot == jnp.broadcast_to(wide_rank[j : j + 1, :], pack_slot.shape)),
                1.0,
                0.0,
            )
            for j in range(dp_count)
        ],
        axis=0,
    ).astype(BF16)

    for a, ref in enumerate((tokens_ref, grads_ref)):
        inputs[2 + a].wait()
        stacked = jnp.concatenate(
            [ref[:, n * LANES : (n + 1) * LANES] for n in range(groups)], axis=0
        )
        zsend[a] = dot(select, stacked, NN).astype(BF16).reshape(dp_count, packed, LANES)
        zrecv[a, plane] = zsend[a, plane]
        if a == 0:
            aux_recv[plane] = aux_send[plane]
            pl.semaphore_wait(barrier, 4 + dp_count - 1)
        for step in range(1, dp_count):
            other, device = at_plane(step)
            send(
                zsend.at[a, other],
                zrecv.at[a, plane],
                z_send_sem.at[a, step],
                z_recv_sem.at[a, plane],
                device,
            )
    for step in range(1, dp_count):
        other, device = at_plane(step)
        send(
            aux_send.at[other],
            aux_recv.at[plane],
            aux_send_sem.at[step],
            aux_recv_sem.at[plane],
            device,
        )

    fetch_weights(order[2:6])

    def shift_of(shape, axis):
        slot = lax.broadcasted_iota(jnp.int32, shape, axis)
        return slot, slot + (packed - CAP) * steps_of(slot, CAP, dp_count)

    slot_index, slot_base = shift_of((slots, dp_count * packed), 0)
    packed_index = lax.broadcasted_iota(jnp.int32, (slots, dp_count * packed), 1)
    unpack = [
        jnp.where(packed_index == slot_base + CAP * n, 1.0, 0.0).astype(BF16) for n in range(groups)
    ]
    for a in range(2):
        for step in range(1, dp_count):
            other = (plane + step) % dp_count
            arrived(zrecv.at[a, other], z_send_sem.at[a, step], z_recv_sem.at[a, other])
        received = zrecv[a].reshape(dp_count * packed, LANES)
        for n in range(groups):
            xbuf[a, h, :, n * LANES : (n + 1) * LANES] = dot(unpack[n], received, NN).astype(BF16)
        for slot, partner in enumerate((hx, hy, sib)):
            send(
                xbuf.at[a, h],
                xbuf.at[a, h],
                x_send.at[a, slot],
                x_recv.at[a, h],
                at_hidden(partner),
            )

    fetch_weights(order[6:])

    def wait_x(a, index):
        arrived(xbuf.at[a, index], x_send.at[a, 0], x_recv.at[a, index])

    def forward(a, index, partner, slot):
        send(
            xbuf.at[a, index],
            xbuf.at[a, index],
            x_send.at[a, slot],
            x_recv.at[a, index],
            at_hidden(partner),
        )

    def project(which, index, start):
        weight_copy(which, index).wait()
        left = xbuf[0 if which < 2 else 1, index]
        for begin, size in strips(units, 2 * LANES):
            part = dot(left, weights[which, index, begin : begin + size, :], NT)
            if not start:
                part = part + acc[which, :, begin : begin + size]
            acc[which, :, begin : begin + size] = part

    def project_all(index):
        for which in range(3):
            project(which, index, False)

    project(0, h, True)
    project(1, h, True)
    wait_x(0, hx)
    forward(0, hx, hy, 3)
    forward(0, hx, sib, 4)
    wait_x(0, hy)
    forward(0, hy, sib, 5)
    project(2, h, True)
    wait_x(1, hy)
    forward(1, hy, hx, 3)
    forward(1, hy, sib, 4)
    wait_x(1, hx)
    forward(1, hx, sib, 5)
    wait_x(0, sib)
    wait_x(1, sib)
    project_all(sib)
    project_all(hx)
    wait_x(0, hd)
    forward(0, hd, sib, 6)
    wait_x(1, hd)
    forward(1, hd, sib, 6)
    project_all(hy)
    for index in (hx + to_sib, hy + to_sib):
        wait_x(0, index)
        wait_x(1, index)
        project_all(index)
    project_all(hd)
    wait_x(0, hd + to_sib)
    wait_x(1, hd + to_sib)
    project_all(hd + to_sib)
    x_copy = pltpu.make_async_copy(xbuf.at[0], x_out, out_sem.at[0])
    x_copy.start()

    for step in range(1, dp_count):
        other = (plane + step) % dp_count
        arrived(aux_recv.at[other], aux_send_sem.at[step], aux_recv_sem.at[other])
    slot_value = lax.broadcasted_iota(jnp.int32, (slots, rows), 0).astype(F32)
    slot_prob = jnp.zeros((slots, 1), F32)
    for source in range(dp_count):
        source_rank = jnp.broadcast_to(aux_recv[source, 0:1, 0:rows], (slots, rows))
        source_prob = jnp.broadcast_to(aux_recv[source, 1:2, 0:rows], (slots, rows))
        hit = (source_rank >= 0.0) & (slot_value == source_rank + float(CAP * source))
        slot_prob = slot_prob + jnp.sum(jnp.where(hit, source_prob, 0.0), axis=1, keepdims=True)

    router = jnp.zeros((slots, LANES), F32)
    slot_prob = jnp.broadcast_to(slot_prob, (slots, LANES))
    for begin, size in strips(units, LANES):
        part = slice(begin, begin + size)
        gate_pre = acc[0, :, part]
        up_pre = acc[1, :, part]
        back_pre = acc[2, :, part]
        sigmoid_gate = jax.nn.sigmoid(gate_pre)
        silu_gate = gate_pre * sigmoid_gate
        scaled = slot_prob * back_pre
        dbuf[0, :, part] = (
            scaled * up_pre * sigmoid_gate * (1.0 + gate_pre * (1.0 - sigmoid_gate))
        ).astype(BF16)
        dbuf[1, :, part] = (scaled * silu_gate).astype(BF16)
        router = router + silu_gate * up_pre * back_pre
    d_copy = pltpu.make_async_copy(dbuf, d_out, out_sem.at[1])
    d_copy.start()
    router = jnp.broadcast_to(jnp.sum(router, axis=1, keepdims=True), (slots, LANES))
    if slots < LANES:
        router = jnp.concatenate([router, jnp.zeros((LANES - slots, LANES), F32)], axis=0)
    q_send[0] = router.T[0:8, :]
    send(q_send.at[0], q_recv.at[0], q_send_sem.at[0], q_recv_sem.at[0], at_hidden(sib))

    column_strips = strips(width, 2 * LANES)

    def partial(index, begin, size):
        part = slice(begin, begin + size)
        return dot(dbuf[0], weights[0, index, :, part], NN) + dot(
            dbuf[1], weights[1, index, :, part], NN
        )

    chips = (hd, hx, hy, h)

    def sibling_part(slot):
        for begin, size in column_strips:
            one_send[slot, :, begin : begin + size] = partial(
                chips[slot] + to_sib, begin, size
            ).astype(BF16)
        send(
            one_send.at[slot],
            one_recv.at[slot],
            one_send_sem.at[slot],
            one_recv_sem.at[slot],
            at_hidden(sib),
        )

    sibling_part(0)
    arrived(q_recv.at[0], q_send_sem.at[0], q_recv_sem.at[0])
    q_send[1] = q_send[0] + q_recv[0]
    for slot, index in enumerate((hd, hx, hy)):
        send(
            q_send.at[1],
            q_recv.at[1 + slot],
            q_send_sem.at[1 + slot],
            q_recv_sem.at[1 + slot],
            at_hidden(index),
        )
    for slot, index in enumerate(chips):
        if slot < 3:
            sibling_part(slot + 1)
        for begin, size in column_strips:
            own_part[:, begin : begin + size] = partial(index, begin, size)
        arrived(one_recv.at[slot], one_send_sem.at[slot], one_recv_sem.at[slot])
        total = own_part[...] + one_recv[slot].astype(F32)
        if slot == 3:
            own_part[...] = total
        else:
            two_send[slot] = total.astype(BF16)
            send(
                two_send.at[slot],
                two_recv.at[slot],
                two_send_sem.at[slot],
                two_recv_sem.at[slot],
                at_hidden(index),
            )

    for slot in range(3):
        arrived(q_recv.at[1 + slot], q_send_sem.at[1 + slot], q_recv_sem.at[1 + slot])
    q_total = (q_send[1] + q_recv[2]) + (q_recv[3] + q_recv[1])
    qz_send[...] = q_total
    qz_recv[plane] = q_total
    for step in range(1, dp_count):
        _, device = at_plane(step)
        send(qz_send, qz_recv.at[plane], qz_send_sem.at[step], qz_recv_sem.at[plane], device)

    for slot in range(3):
        arrived(two_recv.at[slot], two_send_sem.at[slot], two_recv_sem.at[slot])
    features = (
        own_part[...]
        + two_recv[0].astype(F32)
        + two_recv[1].astype(F32)
        + two_recv[2].astype(F32)
    ).astype(BF16)
    _, slot_base = shift_of((dp_count * packed, slots), 1)
    packed_index = lax.broadcasted_iota(jnp.int32, (dp_count * packed, slots), 0)
    returned = jnp.zeros((dp_count * packed, LANES), F32)
    for n in range(groups):
        place = jnp.where(packed_index == slot_base + CAP * n, 1.0, 0.0).astype(BF16)
        returned = returned + dot(place, features[:, n * LANES : (n + 1) * LANES], NN)
    back_send[...] = returned.astype(BF16).reshape(dp_count, packed, LANES)
    back_recv[plane] = back_send[plane]
    for step in range(1, dp_count):
        other, device = at_plane(step)
        send(
            back_send.at[other],
            back_recv.at[plane],
            back_send_sem.at[step],
            back_recv_sem.at[plane],
            device,
        )

    for step in range(1, dp_count):
        other = (plane + step) % dp_count
        arrived(qz_recv.at[other], qz_send_sem.at[step], qz_recv_sem.at[other])
    q_rows = jnp.concatenate(
        [qz_recv[j, 0:1, :] for j in range(dp_count)] + [jnp.zeros((LANES - dp_count, LANES), F32)],
        axis=0,
    )
    q_columns = q_rows.T
    wanted = lax.broadcasted_iota(jnp.int32, (LANES, rows), 0).astype(F32) - (CAP * plane).astype(F32)
    found = [jnp.zeros((1, rows), F32), jnp.zeros((1, rows), F32)]
    for j, owner in enumerate(owners):
        hit = (wanted == jnp.broadcast_to(rank[j : j + 1, :], wanted.shape)) & (wanted >= 0.0)
        column = jnp.broadcast_to(q_columns[:, j : j + 1], wanted.shape)
        value = jnp.sum(jnp.where(hit, column, 0.0), axis=0, keepdims=True)
        for k in range(2):
            found[k] = found[k] + jnp.where(routes_ref[k : k + 1, :] == owner, value, 0.0)
    grad_probs_ref[...] = jnp.concatenate(found, axis=0)

    for step in range(1, dp_count):
        other = (plane + step) % dp_count
        arrived(back_recv.at[other], back_send_sem.at[step], back_recv_sem.at[other])
    stacked = dot(select, back_recv[...].reshape(dp_count * packed, LANES), TN)
    for n in range(groups):
        grad_tokens_ref[:, n * LANES : (n + 1) * LANES] = stacked[n * rows : (n + 1) * rows, :].astype(
            BF16
        )

    for copy in pending:
        copy.wait_send()
    x_copy.wait()
    d_copy.wait()


def outer_kernel(d_ref, x_ref, tokens_ref, probs_ref, gate_ref, up_ref, tokens_out, probs_out):
    width = x_ref.shape[2]
    for which, out in enumerate((gate_ref, up_ref)):
        left = d_ref[which].astype(F32).T.astype(BF16)
        for index in range(x_ref.shape[0]):
            for begin, size in strips(width, 2 * LANES):
                start = index * width + begin
                out[:, start : start + size] = dot(
                    left, x_ref[index, :, begin : begin + size], NN
                ).astype(BF16)

    @pl.when(pl.program_id(0) == 0)
    def _():
        tokens_out[...] = tokens_ref[...]
        probs_out[...] = probs_ref[...]


def fused_body(dp_count, tokens, grad_out, routes, probs, gate_weight, up_weight, down_weight):
    rows, width = tokens.shape
    units, model = gate_weight.shape
    hidden_count = model // width
    groups = width // LANES
    packed = CAP * groups
    slots = CAP * dp_count
    large_count = dp_count // 6
    owners = tuple(j // 4 if j < 4 * large_count else j - 3 * large_count for j in range(dp_count))
    dma = pltpu.SemaphoreType.DMA
    vmem = pl.BlockSpec(memory_space=pltpu.VMEM)
    anywhere = pl.BlockSpec(memory_space=pl.ANY)
    grad_tokens, grad_probs, x_all, d_all = pl.pallas_call(
        functools.partial(fused_kernel, dp_count, owners),
        out_shape=(
            jax.ShapeDtypeStruct((rows, width), BF16),
            jax.ShapeDtypeStruct((2, rows), F32),
            jax.ShapeDtypeStruct((hidden_count, slots, width), BF16),
            jax.ShapeDtypeStruct((2, slots, units), BF16),
        ),
        in_specs=[pl.BlockSpec(memory_space=pltpu.HBM)] * 7,
        out_specs=(vmem, vmem, anywhere, anywhere),
        scratch_shapes=[
            pltpu.VMEM((3, hidden_count, units, width), BF16),
            dma((3, hidden_count)),
            pltpu.VMEM((2, hidden_count, slots, width), BF16),
            dma((2, 7)),
            dma((2, hidden_count)),
            pltpu.VMEM((2, dp_count, packed, LANES), BF16),
            pltpu.VMEM((2, dp_count, packed, LANES), BF16),
            dma((2, dp_count)),
            dma((2, dp_count)),
            pltpu.VMEM((dp_count, 8, LANES), F32),
            pltpu.VMEM((dp_count, 8, LANES), F32),
            dma((dp_count,)),
            dma((dp_count,)),
            pltpu.VMEM((3, slots, units), F32),
            pltpu.VMEM((2, slots, units), BF16),
            pltpu.VMEM((4, slots, width), BF16),
            pltpu.VMEM((4, slots, width), BF16),
            dma((4,)),
            dma((4,)),
            pltpu.VMEM((3, slots, width), BF16),
            pltpu.VMEM((3, slots, width), BF16),
            dma((3,)),
            dma((3,)),
            pltpu.VMEM((slots, width), F32),
            pltpu.VMEM((2, 8, LANES), F32),
            pltpu.VMEM((4, 8, LANES), F32),
            dma((4,)),
            dma((4,)),
            pltpu.VMEM((dp_count, packed, LANES), BF16),
            pltpu.VMEM((dp_count, packed, LANES), BF16),
            dma((dp_count,)),
            dma((dp_count,)),
            pltpu.VMEM((8, LANES), F32),
            pltpu.VMEM((dp_count, 8, LANES), F32),
            dma((dp_count,)),
            dma((dp_count,)),
            dma((2,)),
            pltpu.VMEM((2, rows), jnp.int32),
            pltpu.VMEM((2, rows), BF16),
            pltpu.VMEM((rows, width), BF16),
            pltpu.VMEM((rows, width), BF16),
            dma((4,)),
        ],
        compiler_params=pltpu.CompilerParams(
            collective_id=0, has_side_effects=True, vmem_limit_bytes=64 << 20
        ),
    )(routes.T, probs.T, tokens, grad_out, gate_weight, up_weight, down_weight)
    grad_gate, grad_up, grad_tokens, grad_probs = pl.pallas_call(
        outer_kernel,
        grid=(units // LANES,),
        out_shape=(
            jax.ShapeDtypeStruct((units, model), BF16),
            jax.ShapeDtypeStruct((units, model), BF16),
            jax.ShapeDtypeStruct((rows, width), BF16),
            jax.ShapeDtypeStruct((2, rows), F32),
        ),
        in_specs=[
            pl.BlockSpec((2, slots, LANES), lambda i: (0, 0, i)),
            pl.BlockSpec((hidden_count, slots, width), lambda i: (0, 0, 0)),
            pl.BlockSpec((rows, width), lambda i: (0, 0)),
            pl.BlockSpec((2, rows), lambda i: (0, 0)),
        ],
        out_specs=(
            pl.BlockSpec((LANES, model), lambda i: (i, 0)),
            pl.BlockSpec((LANES, model), lambda i: (i, 0)),
            pl.BlockSpec((rows, width), lambda i: (0, 0)),
            pl.BlockSpec((2, rows), lambda i: (0, 0)),
        ),
        compiler_params=pltpu.CompilerParams(vmem_limit_bytes=64 << 20),
    )(d_all, x_all, grad_tokens, grad_probs)
    return (grad_tokens, grad_probs.T, grad_gate, grad_up)


def solution(mesh):
    placed = (
        P("dp", "hidden"),
        P("dp", "hidden"),
        P("dp", None),
        P("dp", None),
        P(("dp", "hidden"), None),
        P(("dp", "hidden"), None),
        P(("dp", "hidden"), None),
    )

    def local(tokens, grad_out, routes, probs, gate_weight, up_weight, down_weight):
        args = (tokens, grad_out, routes, probs, gate_weight, up_weight, down_weight)
        if fits(mesh.shape["dp"], mesh.shape["hidden"], tokens.shape, gate_weight.shape):
            return fused_body(mesh.shape["dp"], *args)
        return body(*args)

    return jax.shard_map(
        local,
        mesh=mesh,
        in_specs=placed,
        out_specs=(
            P("dp", "hidden"),
            P("dp", None),
            P(("dp", "hidden"), None),
            P(("dp", "hidden"), None),
        ),
        check_vma=False,
    )
```

```python
import functools

import jax
import jax.numpy as jnp
from jax import lax
from jax.experimental import pallas as pl
from jax.experimental.pallas import tpu as pltpu
from jax.sharding import PartitionSpec as P

CAP = 20


def body(tokens, grad_out, routes, probs, gate_weight, up_weight, down_weight):
    dp_count = lax.axis_size("dp")
    hidden_count = lax.axis_size("hidden")
    large_count = dp_count // 6
    expert_total = dp_count - 3 * large_count
    block_ids = jnp.arange(dp_count, dtype=jnp.int32)
    owners = jnp.where(block_ids < 4 * large_count, block_ids // 4, block_ids - 3 * large_count)
    expert_hits = (
        routes[:, :, None] == jnp.arange(expert_total, dtype=jnp.int32)[None, None, :]
    ).astype(jnp.int32)
    per_token = jnp.sum(expert_hits, axis=1)
    before = jnp.cumsum(per_token, axis=0) - per_token
    slot_rank = jnp.sum(expert_hits * before[:, None, :], axis=2)
    matches = routes[:, :, None] == owners[None, None, :]
    slot_hits = slot_rank[:, :, None, None] == jnp.arange(CAP, dtype=jnp.int32)[None, None, None, :]
    picked = (matches[:, :, :, None] & slot_hits).astype(jnp.float32)
    select = jnp.sum(picked, axis=1)
    select_half = select.astype(jnp.bfloat16)
    send_tokens = jnp.einsum(
        "tjc,td->jcd", select_half, tokens, preferred_element_type=jnp.float32
    ).astype(jnp.bfloat16)
    send_grads = jnp.einsum(
        "tjc,td->jcd", select_half, grad_out, preferred_element_type=jnp.float32
    ).astype(jnp.bfloat16)
    send_probs = jnp.einsum(
        "tkjc,tk->jc", picked, probs.astype(jnp.float32), precision=lax.Precision.HIGHEST
    ).astype(jnp.bfloat16)
    recv_tokens, recv_grads, recv_probs = (
        lax.all_to_all(send_tokens, "dp", split_axis=0, concat_axis=0, tiled=True),
        lax.all_to_all(send_grads, "dp", split_axis=0, concat_axis=0, tiled=True),
        lax.all_to_all(send_probs, "dp", split_axis=0, concat_axis=0, tiled=True),
    )
    row_count = dp_count * CAP
    contract = (((1,), (1,)), ((), ()))
    full_tokens, full_grads = (
        lax.all_gather(recv_tokens, "hidden", axis=2, tiled=True),
        lax.all_gather(recv_grads, "hidden", axis=2, tiled=True),
    )
    token_rows = full_tokens.reshape(row_count, full_tokens.shape[2])
    grad_rows = full_grads.reshape(row_count, full_grads.shape[2])
    back_pre = lax.dot_general(grad_rows, down_weight, contract, preferred_element_type=jnp.float32)
    slot_probs = recv_probs.reshape(row_count).astype(jnp.float32)
    gate_pre = lax.dot_general(
        token_rows, gate_weight, contract, preferred_element_type=jnp.float32
    )
    up_pre = lax.dot_general(token_rows, up_weight, contract, preferred_element_type=jnp.float32)
    sigmoid_gate = jax.nn.sigmoid(gate_pre)
    silu_gate = gate_pre * sigmoid_gate
    router_part = jnp.sum(silu_gate * up_pre * back_pre, axis=1)
    scaled = slot_probs[:, None] * back_pre
    grad_gate_pre = (
        scaled * up_pre * sigmoid_gate * (1.0 + gate_pre * (1.0 - sigmoid_gate))
    ).astype(jnp.bfloat16)
    grad_up_pre = (scaled * silu_gate).astype(jnp.bfloat16)
    over_rows = (((0,), (0,)), ((), ()))
    grad_gate = lax.dot_general(
        grad_gate_pre, token_rows, over_rows, preferred_element_type=jnp.float32
    ).astype(jnp.bfloat16)
    grad_up = lax.dot_general(
        grad_up_pre, token_rows, over_rows, preferred_element_type=jnp.float32
    ).astype(jnp.bfloat16)
    feature_width = gate_weight.shape[1] // hidden_count
    cross = (((0,), (1,)), ((), ()))
    own_features = lax.psum_scatter(
        lax.dot_general(gate_weight, grad_gate_pre, cross, preferred_element_type=jnp.float32)
        + lax.dot_general(up_weight, grad_up_pre, cross, preferred_element_type=jnp.float32),
        "hidden",
        scatter_dimension=0,
        tiled=True,
    ).T
    router_payload = lax.psum(router_part, "hidden")
    back_features, back_router = (
        lax.all_to_all(
            own_features.reshape(dp_count, CAP, feature_width),
            "dp",
            split_axis=0,
            concat_axis=0,
            tiled=True,
        ),
        lax.all_to_all(
            router_payload.reshape(dp_count, CAP), "dp", split_axis=0, concat_axis=0, tiled=True
        ),
    )
    token_router = jnp.einsum("tkjc,jc->tk", picked, back_router, precision=lax.Precision.HIGHEST)
    grad_tokens = jnp.einsum(
        "tjc,jcd->td", select, back_features, precision=lax.Precision.HIGHEST
    ).astype(jnp.bfloat16)
    return (grad_tokens, token_router, grad_gate, grad_up)


LANES = 128
MESH = pl.DeviceIdType.MESH
F32 = jnp.float32
BF16 = jnp.bfloat16
NT = (((1,), (1,)), ((), ()))
NN = (((1,), (0,)), ((), ()))
TN = (((0,), (0,)), ((), ()))


def fits(dp_count, hidden_count, token_shape, weight_shape):
    rows, width = token_shape
    groups = width // LANES
    return (
        hidden_count == 8
        and 2 <= dp_count <= 8
        and width % LANES == 0
        and rows * groups == LANES
        and (CAP * groups) % 16 == 0
        and (CAP * dp_count) % 16 == 0
        and CAP * dp_count <= LANES
        and weight_shape[0] % LANES == 0
    )


def dot(a, b, dims):
    return lax.dot_general(a, b, dims, preferred_element_type=F32)


def strips(total, size):
    return [(start, min(size, total - start)) for start in range(0, total, size)]


def steps_of(values, size, count):
    total = jnp.zeros_like(values)
    for edge in range(1, count):
        total = total + (values >= edge * size).astype(jnp.int32)
    return total


def fused_kernel(
    dp_count,
    owners,
    routes_hbm,
    probs_hbm,
    tokens_hbm,
    grads_hbm,
    gate_hbm,
    up_hbm,
    down_hbm,
    grad_tokens_ref,
    grad_probs_ref,
    x_out,
    d_out,
    weights,
    weight_sem,
    xbuf,
    x_send,
    x_recv,
    zsend,
    zrecv,
    z_send_sem,
    z_recv_sem,
    aux_send,
    aux_recv,
    aux_send_sem,
    aux_recv_sem,
    acc,
    router_sum,
    dbuf,
    one_send,
    one_recv,
    one_send_sem,
    one_recv_sem,
    two_send,
    two_recv,
    two_send_sem,
    two_recv_sem,
    own_part,
    q_send,
    q_recv,
    q_send_sem,
    q_recv_sem,
    back_send,
    back_recv,
    back_send_sem,
    back_recv_sem,
    qz_send,
    qz_recv,
    qz_send_sem,
    qz_recv_sem,
    out_sem,
    routes_ref,
    probs_ref,
    tokens_ref,
    grads_ref,
    in_sem,
):
    rows, width = tokens_ref.shape
    units = gate_hbm.shape[0]
    groups = width // LANES
    packed = CAP * groups
    slots = CAP * dp_count
    plane = lax.axis_index("dp")
    h = lax.axis_index("hidden")
    core = h % 2
    x_pos = (h // 2) % 2
    y_pos = h // 4
    to_sib = 1 - 2 * core
    sib = h + to_sib
    hx = h + 2 - 4 * x_pos
    hy = h + 4 - 8 * y_pos
    hd = hx + 4 - 8 * y_pos

    def chip_at(flip_x, flip_y):
        return h + flip_x * (2 - 4 * x_pos) + flip_y * (4 - 8 * y_pos)

    def at_hidden(index):
        return (plane, index)

    def at_plane(step):
        other = (plane + step) % dp_count
        return other, (other, h)

    inputs = [
        pltpu.make_async_copy(source, target, in_sem.at[n])
        for n, (source, target) in enumerate(
            (
                (routes_hbm, routes_ref),
                (probs_hbm, probs_ref),
                (tokens_hbm, tokens_ref),
                (grads_hbm, grads_ref),
            )
        )
    ]
    for copy in inputs:
        copy.start()

    barrier = pltpu.get_barrier_semaphore()
    for index in (sib, hx, hy, hd):
        pl.semaphore_signal(barrier, inc=1, device_id=at_hidden(index), device_id_type=MESH)
    for step in range(1, dp_count):
        pl.semaphore_signal(barrier, inc=1, device_id=at_plane(step)[1], device_id_type=MESH)

    order = (h, sib, hx, hx + to_sib, hy, hy + to_sib, hd, hd + to_sib)

    def weight_copy(which, index):
        columns = pl.ds(pl.multiple_of(index * width, width), width)
        source = (gate_hbm, up_hbm, down_hbm)[which]
        return pltpu.make_async_copy(
            source.at[:, columns], weights.at[which, index], weight_sem.at[which, index]
        )

    def fetch_weights(indices):
        for index in indices:
            for which in range(3):
                weight_copy(which, index).start()

    fetch_weights(order[:2])
    pending = []

    def start(source, target, send_sem, recv_sem, device):
        pltpu.make_async_remote_copy(
            src_ref=source,
            dst_ref=target,
            send_sem=send_sem,
            recv_sem=recv_sem,
            device_id=device,
            device_id_type=MESH,
        ).start()

    def send(source, target, send_sem, recv_sem, device):
        start(source, target, send_sem, recv_sem, device)
        pending.append((source, send_sem))

    def arrived(target, send_sem, recv_sem):
        pltpu.make_async_remote_copy(
            src_ref=target,
            dst_ref=target,
            send_sem=send_sem,
            recv_sem=recv_sem,
            device_id=at_hidden(sib),
            device_id_type=MESH,
        ).wait_recv()

    block_row = lax.broadcasted_iota(jnp.int32, (8, rows), 0)
    owner_of = jnp.full((8, rows), -1, jnp.int32)
    for j, owner in enumerate(owners):
        owner_of = jnp.where(block_row == j, owner, owner_of)
    inputs[0].wait()
    inputs[1].wait()
    first = jnp.broadcast_to(routes_ref[0:1, :], (8, rows))
    second = jnp.broadcast_to(routes_ref[1:2, :], (8, rows))
    prob_rows = probs_ref[...].astype(F32)
    match = (owner_of == first) | (owner_of == second)
    earlier = lax.broadcasted_iota(jnp.int32, (rows, rows), 0) < lax.broadcasted_iota(
        jnp.int32, (rows, rows), 1
    )
    rank = dot(match.astype(F32).astype(BF16), earlier.astype(F32).astype(BF16), NN)
    rank = jnp.where(match, rank, -1.0)
    block_prob = jnp.where(owner_of == first, jnp.broadcast_to(prob_rows[0:1, :], (8, rows)), 0.0)
    block_prob = block_prob + jnp.where(
        owner_of == second, jnp.broadcast_to(prob_rows[1:2, :], (8, rows)), 0.0
    )
    for j in range(dp_count):
        aux_send[j] = jnp.zeros((8, LANES), F32)
        aux_send[j, 0:1, 0:rows] = rank[j : j + 1, :]
        aux_send[j, 1:2, 0:rows] = block_prob[j : j + 1, :]
    wide_rank = jnp.concatenate([rank] * groups, axis=1)
    pack_row = lax.broadcasted_iota(jnp.int32, (packed, LANES), 0)
    pack_group = steps_of(pack_row, CAP, groups)
    pack_slot = (pack_row - CAP * pack_group).astype(F32)
    lane_group = steps_of(lax.broadcasted_iota(jnp.int32, (packed, LANES), 1), rows, groups)
    same_group = pack_group == lane_group
    select = jnp.concatenate(
        [
            jnp.where(
                same_group & (pack_slot == jnp.broadcast_to(wide_rank[j : j + 1, :], pack_slot.shape)),
                1.0,
                0.0,
            )
            for j in range(dp_count)
        ],
        axis=0,
    ).astype(BF16)

    for a, ref in enumerate((tokens_ref, grads_ref)):
        inputs[2 + a].wait()
        stacked = jnp.concatenate(
            [ref[:, n * LANES : (n + 1) * LANES] for n in range(groups)], axis=0
        )
        zsend[a] = dot(select, stacked, NN).astype(BF16).reshape(dp_count, packed, LANES)
        zrecv[a, plane] = zsend[a, plane]
        if a == 0:
            aux_recv[plane] = aux_send[plane]
            pl.semaphore_wait(barrier, 4 + dp_count - 1)
        for step in range(1, dp_count):
            other, device = at_plane(step)
            send(
                zsend.at[a, other],
                zrecv.at[a, plane],
                z_send_sem.at[a, step],
                z_recv_sem.at[a, plane],
                device,
            )
    for step in range(1, dp_count):
        other, device = at_plane(step)
        send(
            aux_send.at[other],
            aux_recv.at[plane],
            aux_send_sem.at[step],
            aux_recv_sem.at[plane],
            device,
        )

    fetch_weights(order[2:6])

    def shift_of(shape, axis):
        slot = lax.broadcasted_iota(jnp.int32, shape, axis)
        return slot, slot + (packed - CAP) * steps_of(slot, CAP, dp_count)

    slot_index, slot_base = shift_of((slots, dp_count * packed), 0)
    packed_index = lax.broadcasted_iota(jnp.int32, (slots, dp_count * packed), 1)
    unpack = [
        jnp.where(packed_index == slot_base + CAP * n, 1.0, 0.0).astype(BF16) for n in range(groups)
    ]
    for a in range(2):
        for step in range(1, dp_count):
            other = (plane + step) % dp_count
            arrived(zrecv.at[a, other], z_send_sem.at[a, step], z_recv_sem.at[a, other])
        received = zrecv[a].reshape(dp_count * packed, LANES)
        for n in range(groups):
            xbuf[a, h, :, n * LANES : (n + 1) * LANES] = dot(unpack[n], received, NN).astype(BF16)
        for slot, partner in enumerate((hx, hy, sib)):
            send(
                xbuf.at[a, h],
                xbuf.at[a, h],
                x_send.at[a, slot],
                x_recv.at[a, h],
                at_hidden(partner),
            )

    fetch_weights(order[6:])

    def wait_x(a, index):
        arrived(xbuf.at[a, index], x_send.at[a, 0], x_recv.at[a, index])

    def forward(a, index, partner, slot):
        start(
            xbuf.at[a, index],
            xbuf.at[a, index],
            x_send.at[a, slot],
            x_recv.at[a, index],
            at_hidden(partner),
        )

    acc[...] = jnp.zeros_like(acc)

    @pl.loop(0, 8)
    def _(i):
        @pl.when(i == 1)
        def _():
            wait_x(0, hx)
            forward(0, hx, hy, 3)
            forward(0, hx, sib, 4)
            wait_x(0, hy)
            forward(0, hy, sib, 5)
            wait_x(0, sib)
            wait_x(1, sib)

        @pl.when(i == 2)
        def _():
            wait_x(1, hy)
            forward(1, hy, hx, 3)
            forward(1, hy, sib, 4)
            wait_x(1, hx)
            forward(1, hx, sib, 5)

        @pl.when(i == 3)
        def _():
            wait_x(0, hx + to_sib)
            wait_x(1, hx + to_sib)

        @pl.when(i == 5)
        def _():
            wait_x(0, hd)
            forward(0, hd, sib, 6)
            wait_x(1, hd)
            forward(1, hd, sib, 6)
            wait_x(0, hy + to_sib)
            wait_x(1, hy + to_sib)

        @pl.when(i == 7)
        def _():
            wait_x(0, hd + to_sib)
            wait_x(1, hd + to_sib)

        index = chip_at((i // 2) % 2, i // 4) + (i % 2) * to_sib
        for which in range(3):
            weight_copy(which, index).wait()
            left = xbuf[0 if which < 2 else 1, index]
            for begin, size in strips(units, 2 * LANES):
                acc[which, :, begin : begin + size] += dot(
                    left, weights[which, index, begin : begin + size, :], NT
                )

    x_copy = pltpu.make_async_copy(xbuf.at[0], x_out, out_sem.at[0])
    x_copy.start()

    for step in range(1, dp_count):
        other = (plane + step) % dp_count
        arrived(aux_recv.at[other], aux_send_sem.at[step], aux_recv_sem.at[other])
    slot_value = lax.broadcasted_iota(jnp.int32, (slots, rows), 0).astype(F32)
    slot_prob = jnp.zeros((slots, 1), F32)
    for source in range(dp_count):
        source_rank = jnp.broadcast_to(aux_recv[source, 0:1, 0:rows], (slots, rows))
        source_prob = jnp.broadcast_to(aux_recv[source, 1:2, 0:rows], (slots, rows))
        hit = (source_rank >= 0.0) & (slot_value == source_rank + float(CAP * source))
        slot_prob = slot_prob + jnp.sum(jnp.where(hit, source_prob, 0.0), axis=1, keepdims=True)

    slot_prob = jnp.broadcast_to(slot_prob, (slots, LANES))
    router_sum[...] = jnp.zeros_like(router_sum)

    @pl.loop(0, units // LANES)
    def _(i):
        part = pl.ds(pl.multiple_of(i * LANES, LANES), LANES)
        gate_pre = acc[0, :, part]
        up_pre = acc[1, :, part]
        back_pre = acc[2, :, part]
        sigmoid_gate = jax.nn.sigmoid(gate_pre)
        silu_gate = gate_pre * sigmoid_gate
        scaled = slot_prob * back_pre
        dbuf[0, :, part] = (
            scaled * up_pre * sigmoid_gate * (1.0 + gate_pre * (1.0 - sigmoid_gate))
        ).astype(BF16)
        dbuf[1, :, part] = (scaled * silu_gate).astype(BF16)
        router_sum[...] += silu_gate * up_pre * back_pre

    d_copy = pltpu.make_async_copy(dbuf, d_out, out_sem.at[1])
    d_copy.start()
    router = jnp.broadcast_to(jnp.sum(router_sum[...], axis=1, keepdims=True), (slots, LANES))
    if slots < LANES:
        router = jnp.concatenate([router, jnp.zeros((LANES - slots, LANES), F32)], axis=0)
    q_send[0] = router.T[0:8, :]
    send(q_send.at[0], q_recv.at[0], q_send_sem.at[0], q_recv_sem.at[0], at_hidden(sib))

    column_strips = strips(width, 2 * LANES)

    def partial(index, begin, size):
        part = slice(begin, begin + size)
        return dot(dbuf[0], weights[0, index, :, part], NN) + dot(
            dbuf[1], weights[1, index, :, part], NN
        )

    def chip_of(slot):
        return chip_at((3 - slot) // 2, (3 - slot) % 2)

    @pl.loop(0, 5)
    def _(turn):
        @pl.when(turn < 4)
        def _():
            for begin, size in column_strips:
                one_send[turn, :, begin : begin + size] = partial(
                    chip_of(turn) + to_sib, begin, size
                ).astype(BF16)
            start(
                one_send.at[turn],
                one_recv.at[turn],
                one_send_sem.at[turn],
                one_recv_sem.at[turn],
                at_hidden(sib),
            )

        @pl.when(turn == 1)
        def _():
            arrived(q_recv.at[0], q_send_sem.at[0], q_recv_sem.at[0])
            q_send[1] = q_send[0] + q_recv[0]
            for place, index in enumerate((hd, hx, hy)):
                start(
                    q_send.at[1],
                    q_recv.at[1 + place],
                    q_send_sem.at[1 + place],
                    q_recv_sem.at[1 + place],
                    at_hidden(index),
                )

        @pl.when(turn > 0)
        def _():
            slot = turn - 1
            index = chip_of(slot)
            for begin, size in column_strips:
                own_part[:, begin : begin + size] = partial(index, begin, size)
            arrived(one_recv.at[slot], one_send_sem.at[slot], one_recv_sem.at[slot])
            own_part[...] += one_recv[slot].astype(F32)

            @pl.when(slot < 3)
            def _():
                two_send[slot] = own_part[...].astype(BF16)
                start(
                    two_send.at[slot],
                    two_recv.at[slot],
                    two_send_sem.at[slot],
                    two_recv_sem.at[slot],
                    at_hidden(index),
                )

    for a in range(2):
        for slot in range(3, 7):
            pending.append((xbuf.at[a, h], x_send.at[a, slot]))
    for slot in range(3):
        pending.append((q_send.at[1], q_send_sem.at[1 + slot]))
    for slot in range(4):
        pending.append((one_send.at[slot], one_send_sem.at[slot]))
    for slot in range(3):
        pending.append((two_send.at[slot], two_send_sem.at[slot]))

    for slot in range(3):
        arrived(q_recv.at[1 + slot], q_send_sem.at[1 + slot], q_recv_sem.at[1 + slot])
    q_total = (q_send[1] + q_recv[2]) + (q_recv[3] + q_recv[1])
    qz_send[...] = q_total
    qz_recv[plane] = q_total
    for step in range(1, dp_count):
        _, device = at_plane(step)
        send(qz_send, qz_recv.at[plane], qz_send_sem.at[step], qz_recv_sem.at[plane], device)

    for slot in range(3):
        arrived(two_recv.at[slot], two_send_sem.at[slot], two_recv_sem.at[slot])
    features = (
        own_part[...]
        + two_recv[0].astype(F32)
        + two_recv[1].astype(F32)
        + two_recv[2].astype(F32)
    ).astype(BF16)
    _, slot_base = shift_of((dp_count * packed, slots), 1)
    packed_index = lax.broadcasted_iota(jnp.int32, (dp_count * packed, slots), 0)
    returned = jnp.zeros((dp_count * packed, LANES), F32)
    for n in range(groups):
        place = jnp.where(packed_index == slot_base + CAP * n, 1.0, 0.0).astype(BF16)
        returned = returned + dot(place, features[:, n * LANES : (n + 1) * LANES], NN)
    back_send[...] = returned.astype(BF16).reshape(dp_count, packed, LANES)
    back_recv[plane] = back_send[plane]
    for step in range(1, dp_count):
        other, device = at_plane(step)
        send(
            back_send.at[other],
            back_recv.at[plane],
            back_send_sem.at[step],
            back_recv_sem.at[plane],
            device,
        )

    for step in range(1, dp_count):
        other = (plane + step) % dp_count
        arrived(qz_recv.at[other], qz_send_sem.at[step], qz_recv_sem.at[other])
    q_rows = jnp.concatenate(
        [qz_recv[j, 0:1, :] for j in range(dp_count)] + [jnp.zeros((LANES - dp_count, LANES), F32)],
        axis=0,
    )
    q_columns = q_rows.T
    wanted = lax.broadcasted_iota(jnp.int32, (LANES, rows), 0).astype(F32) - (CAP * plane).astype(F32)
    found = [jnp.zeros((1, rows), F32), jnp.zeros((1, rows), F32)]
    for j, owner in enumerate(owners):
        hit = (wanted == jnp.broadcast_to(rank[j : j + 1, :], wanted.shape)) & (wanted >= 0.0)
        column = jnp.broadcast_to(q_columns[:, j : j + 1], wanted.shape)
        value = jnp.sum(jnp.where(hit, column, 0.0), axis=0, keepdims=True)
        for k in range(2):
            found[k] = found[k] + jnp.where(routes_ref[k : k + 1, :] == owner, value, 0.0)
    grad_probs_ref[...] = jnp.concatenate(found, axis=0)

    for step in range(1, dp_count):
        other = (plane + step) % dp_count
        arrived(back_recv.at[other], back_send_sem.at[step], back_recv_sem.at[other])
    stacked = dot(select, back_recv[...].reshape(dp_count * packed, LANES), TN)
    for n in range(groups):
        grad_tokens_ref[:, n * LANES : (n + 1) * LANES] = stacked[n * rows : (n + 1) * rows, :].astype(
            BF16
        )

    for source, send_sem in pending:
        pltpu.make_async_remote_copy(
            src_ref=source,
            dst_ref=source,
            send_sem=send_sem,
            recv_sem=send_sem,
            device_id=at_hidden(sib),
            device_id_type=MESH,
        ).wait_send()
    x_copy.wait()
    d_copy.wait()


def outer_kernel(d_ref, x_ref, tokens_ref, probs_ref, gate_ref, up_ref, tokens_out, probs_out):
    width = x_ref.shape[2]
    for which, out in enumerate((gate_ref, up_ref)):
        left = d_ref[which].astype(F32).T.astype(BF16)
        for index in range(x_ref.shape[0]):
            for begin, size in strips(width, 2 * LANES):
                start = index * width + begin
                out[:, start : start + size] = dot(
                    left, x_ref[index, :, begin : begin + size], NN
                ).astype(BF16)

    @pl.when(pl.program_id(0) == 0)
    def _():
        tokens_out[...] = tokens_ref[...]
        probs_out[...] = probs_ref[...]


def fused_body(dp_count, tokens, grad_out, routes, probs, gate_weight, up_weight, down_weight):
    rows, width = tokens.shape
    units, model = gate_weight.shape
    hidden_count = model // width
    groups = width // LANES
    packed = CAP * groups
    slots = CAP * dp_count
    large_count = dp_count // 6
    owners = tuple(j // 4 if j < 4 * large_count else j - 3 * large_count for j in range(dp_count))
    dma = pltpu.SemaphoreType.DMA
    vmem = pl.BlockSpec(memory_space=pltpu.VMEM)
    anywhere = pl.BlockSpec(memory_space=pl.ANY)
    grad_tokens, grad_probs, x_all, d_all = pl.pallas_call(
        functools.partial(fused_kernel, dp_count, owners),
        out_shape=(
            jax.ShapeDtypeStruct((rows, width), BF16),
            jax.ShapeDtypeStruct((2, rows), F32),
            jax.ShapeDtypeStruct((hidden_count, slots, width), BF16),
            jax.ShapeDtypeStruct((2, slots, units), BF16),
        ),
        in_specs=[pl.BlockSpec(memory_space=pltpu.HBM)] * 7,
        out_specs=(vmem, vmem, anywhere, anywhere),
        scratch_shapes=[
            pltpu.VMEM((3, hidden_count, units, width), BF16),
            dma((3, hidden_count)),
            pltpu.VMEM((2, hidden_count, slots, width), BF16),
            dma((2, 7)),
            dma((2, hidden_count)),
            pltpu.VMEM((2, dp_count, packed, LANES), BF16),
            pltpu.VMEM((2, dp_count, packed, LANES), BF16),
            dma((2, dp_count)),
            dma((2, dp_count)),
            pltpu.VMEM((dp_count, 8, LANES), F32),
            pltpu.VMEM((dp_count, 8, LANES), F32),
            dma((dp_count,)),
            dma((dp_count,)),
            pltpu.VMEM((3, slots, units), F32),
            pltpu.VMEM((slots, LANES), F32),
            pltpu.VMEM((2, slots, units), BF16),
            pltpu.VMEM((4, slots, width), BF16),
            pltpu.VMEM((4, slots, width), BF16),
            dma((4,)),
            dma((4,)),
            pltpu.VMEM((3, slots, width), BF16),
            pltpu.VMEM((3, slots, width), BF16),
            dma((3,)),
            dma((3,)),
            pltpu.VMEM((slots, width), F32),
            pltpu.VMEM((2, 8, LANES), F32),
            pltpu.VMEM((4, 8, LANES), F32),
            dma((4,)),
            dma((4,)),
            pltpu.VMEM((dp_count, packed, LANES), BF16),
            pltpu.VMEM((dp_count, packed, LANES), BF16),
            dma((dp_count,)),
            dma((dp_count,)),
            pltpu.VMEM((8, LANES), F32),
            pltpu.VMEM((dp_count, 8, LANES), F32),
            dma((dp_count,)),
            dma((dp_count,)),
            dma((2,)),
            pltpu.VMEM((2, rows), jnp.int32),
            pltpu.VMEM((2, rows), BF16),
            pltpu.VMEM((rows, width), BF16),
            pltpu.VMEM((rows, width), BF16),
            dma((4,)),
        ],
        compiler_params=pltpu.CompilerParams(
            collective_id=0, has_side_effects=True, vmem_limit_bytes=64 << 20
        ),
    )(routes.T, probs.T, tokens, grad_out, gate_weight, up_weight, down_weight)
    grad_gate, grad_up, grad_tokens, grad_probs = pl.pallas_call(
        outer_kernel,
        grid=(units // LANES,),
        out_shape=(
            jax.ShapeDtypeStruct((units, model), BF16),
            jax.ShapeDtypeStruct((units, model), BF16),
            jax.ShapeDtypeStruct((rows, width), BF16),
            jax.ShapeDtypeStruct((2, rows), F32),
        ),
        in_specs=[
            pl.BlockSpec((2, slots, LANES), lambda i: (0, 0, i)),
            pl.BlockSpec((hidden_count, slots, width), lambda i: (0, 0, 0)),
            pl.BlockSpec((rows, width), lambda i: (0, 0)),
            pl.BlockSpec((2, rows), lambda i: (0, 0)),
        ],
        out_specs=(
            pl.BlockSpec((LANES, model), lambda i: (i, 0)),
            pl.BlockSpec((LANES, model), lambda i: (i, 0)),
            pl.BlockSpec((rows, width), lambda i: (0, 0)),
            pl.BlockSpec((2, rows), lambda i: (0, 0)),
        ),
        compiler_params=pltpu.CompilerParams(vmem_limit_bytes=64 << 20),
    )(d_all, x_all, grad_tokens, grad_probs)
    return (grad_tokens, grad_probs.T, grad_gate, grad_up)


def solution(mesh):
    placed = (
        P("dp", "hidden"),
        P("dp", "hidden"),
        P("dp", None),
        P("dp", None),
        P(("dp", "hidden"), None),
        P(("dp", "hidden"), None),
        P(("dp", "hidden"), None),
    )

    def local(tokens, grad_out, routes, probs, gate_weight, up_weight, down_weight):
        args = (tokens, grad_out, routes, probs, gate_weight, up_weight, down_weight)
        if fits(mesh.shape["dp"], mesh.shape["hidden"], tokens.shape, gate_weight.shape):
            return fused_body(mesh.shape["dp"], *args)
        return body(*args)

    return jax.shard_map(
        local,
        mesh=mesh,
        in_specs=placed,
        out_specs=(
            P("dp", "hidden"),
            P("dp", None),
            P(("dp", "hidden"), None),
            P(("dp", "hidden"), None),
        ),
        check_vma=False,
    )
```

```python
import functools

import jax
import jax.numpy as jnp
from jax import lax
from jax.experimental import pallas as pl
from jax.experimental.pallas import tpu as pltpu
from jax.sharding import PartitionSpec as P

CAP = 20


def body(tokens, grad_out, routes, probs, gate_weight, up_weight, down_weight):
    dp_count = lax.axis_size("dp")
    hidden_count = lax.axis_size("hidden")
    large_count = dp_count // 6
    expert_total = dp_count - 3 * large_count
    block_ids = jnp.arange(dp_count, dtype=jnp.int32)
    owners = jnp.where(block_ids < 4 * large_count, block_ids // 4, block_ids - 3 * large_count)
    expert_hits = (
        routes[:, :, None] == jnp.arange(expert_total, dtype=jnp.int32)[None, None, :]
    ).astype(jnp.int32)
    per_token = jnp.sum(expert_hits, axis=1)
    before = jnp.cumsum(per_token, axis=0) - per_token
    slot_rank = jnp.sum(expert_hits * before[:, None, :], axis=2)
    matches = routes[:, :, None] == owners[None, None, :]
    slot_hits = slot_rank[:, :, None, None] == jnp.arange(CAP, dtype=jnp.int32)[None, None, None, :]
    picked = (matches[:, :, :, None] & slot_hits).astype(jnp.float32)
    select = jnp.sum(picked, axis=1)
    select_half = select.astype(jnp.bfloat16)
    send_tokens = jnp.einsum(
        "tjc,td->jcd", select_half, tokens, preferred_element_type=jnp.float32
    ).astype(jnp.bfloat16)
    send_grads = jnp.einsum(
        "tjc,td->jcd", select_half, grad_out, preferred_element_type=jnp.float32
    ).astype(jnp.bfloat16)
    send_probs = jnp.einsum(
        "tkjc,tk->jc", picked, probs.astype(jnp.float32), precision=lax.Precision.HIGHEST
    ).astype(jnp.bfloat16)
    recv_tokens, recv_grads, recv_probs = (
        lax.all_to_all(send_tokens, "dp", split_axis=0, concat_axis=0, tiled=True),
        lax.all_to_all(send_grads, "dp", split_axis=0, concat_axis=0, tiled=True),
        lax.all_to_all(send_probs, "dp", split_axis=0, concat_axis=0, tiled=True),
    )
    row_count = dp_count * CAP
    contract = (((1,), (1,)), ((), ()))
    full_tokens, full_grads = (
        lax.all_gather(recv_tokens, "hidden", axis=2, tiled=True),
        lax.all_gather(recv_grads, "hidden", axis=2, tiled=True),
    )
    token_rows = full_tokens.reshape(row_count, full_tokens.shape[2])
    grad_rows = full_grads.reshape(row_count, full_grads.shape[2])
    back_pre = lax.dot_general(grad_rows, down_weight, contract, preferred_element_type=jnp.float32)
    slot_probs = recv_probs.reshape(row_count).astype(jnp.float32)
    gate_pre = lax.dot_general(
        token_rows, gate_weight, contract, preferred_element_type=jnp.float32
    )
    up_pre = lax.dot_general(token_rows, up_weight, contract, preferred_element_type=jnp.float32)
    sigmoid_gate = jax.nn.sigmoid(gate_pre)
    silu_gate = gate_pre * sigmoid_gate
    router_part = jnp.sum(silu_gate * up_pre * back_pre, axis=1)
    scaled = slot_probs[:, None] * back_pre
    grad_gate_pre = (
        scaled * up_pre * sigmoid_gate * (1.0 + gate_pre * (1.0 - sigmoid_gate))
    ).astype(jnp.bfloat16)
    grad_up_pre = (scaled * silu_gate).astype(jnp.bfloat16)
    over_rows = (((0,), (0,)), ((), ()))
    grad_gate = lax.dot_general(
        grad_gate_pre, token_rows, over_rows, preferred_element_type=jnp.float32
    ).astype(jnp.bfloat16)
    grad_up = lax.dot_general(
        grad_up_pre, token_rows, over_rows, preferred_element_type=jnp.float32
    ).astype(jnp.bfloat16)
    feature_width = gate_weight.shape[1] // hidden_count
    cross = (((0,), (1,)), ((), ()))
    own_features = lax.psum_scatter(
        lax.dot_general(gate_weight, grad_gate_pre, cross, preferred_element_type=jnp.float32)
        + lax.dot_general(up_weight, grad_up_pre, cross, preferred_element_type=jnp.float32),
        "hidden",
        scatter_dimension=0,
        tiled=True,
    ).T
    router_payload = lax.psum(router_part, "hidden")
    back_features, back_router = (
        lax.all_to_all(
            own_features.reshape(dp_count, CAP, feature_width),
            "dp",
            split_axis=0,
            concat_axis=0,
            tiled=True,
        ),
        lax.all_to_all(
            router_payload.reshape(dp_count, CAP), "dp", split_axis=0, concat_axis=0, tiled=True
        ),
    )
    token_router = jnp.einsum("tkjc,jc->tk", picked, back_router, precision=lax.Precision.HIGHEST)
    grad_tokens = jnp.einsum(
        "tjc,jcd->td", select, back_features, precision=lax.Precision.HIGHEST
    ).astype(jnp.bfloat16)
    return (grad_tokens, token_router, grad_gate, grad_up)


LANES = 128
MESH = pl.DeviceIdType.MESH
F32 = jnp.float32
BF16 = jnp.bfloat16
NT = (((1,), (1,)), ((), ()))
NN = (((1,), (0,)), ((), ()))
TN = (((0,), (0,)), ((), ()))


def fits(dp_count, hidden_count, token_shape, weight_shape):
    rows, width = token_shape
    groups = width // LANES
    return (
        hidden_count == 8
        and 2 <= dp_count <= 8
        and width % LANES == 0
        and rows * groups == LANES
        and (CAP * groups) % 16 == 0
        and (CAP * dp_count) % 16 == 0
        and CAP * dp_count <= LANES
        and weight_shape[0] % LANES == 0
    )


def dot(a, b, dims):
    return lax.dot_general(a, b, dims, preferred_element_type=F32)


def strips(total, size):
    return [(start, min(size, total - start)) for start in range(0, total, size)]


def steps_of(values, size, count):
    total = jnp.zeros_like(values)
    for edge in range(1, count):
        total = total + (values >= edge * size).astype(jnp.int32)
    return total


def fused_kernel(
    dp_count,
    owners,
    in_ref,
    gate_hbm,
    up_hbm,
    down_hbm,
    grad_tokens_ref,
    grad_probs_ref,
    x_out,
    d_out,
    weights,
    weight_sem,
    xbuf,
    x_send,
    x_recv,
    zsend,
    zrecv,
    z_send_sem,
    z_recv_sem,
    aux_send,
    aux_recv,
    aux_send_sem,
    aux_recv_sem,
    acc,
    router_sum,
    dbuf,
    one_send,
    one_recv,
    one_send_sem,
    one_recv_sem,
    two_send,
    two_recv,
    two_send_sem,
    two_recv_sem,
    own_part,
    q_send,
    q_recv,
    q_send_sem,
    q_recv_sem,
    back_send,
    back_recv,
    back_send_sem,
    back_recv_sem,
    qz_send,
    qz_recv,
    qz_send_sem,
    qz_recv_sem,
    out_sem,
):
    width = in_ref.shape[1]
    rows = (in_ref.shape[0] - 16) // 2
    units = gate_hbm.shape[0]
    groups = width // LANES
    packed = CAP * groups
    slots = CAP * dp_count
    plane = lax.axis_index("dp")
    h = lax.axis_index("hidden")
    core = h % 2
    x_pos = (h // 2) % 2
    y_pos = h // 4
    to_sib = 1 - 2 * core
    sib = h + to_sib
    hx = h + 2 - 4 * x_pos
    hy = h + 4 - 8 * y_pos
    hd = hx + 4 - 8 * y_pos

    def chip_at(flip_x, flip_y):
        return h + flip_x * (2 - 4 * x_pos) + flip_y * (4 - 8 * y_pos)

    def at_hidden(index):
        return (plane, index)

    def at_plane(step):
        other = (plane + step) % dp_count
        return other, (other, h)

    barrier = pltpu.get_barrier_semaphore()
    for index in (sib, hx, hy, hd):
        pl.semaphore_signal(barrier, inc=1, device_id=at_hidden(index), device_id_type=MESH)
    for step in range(1, dp_count):
        pl.semaphore_signal(barrier, inc=1, device_id=at_plane(step)[1], device_id_type=MESH)

    order = (h, sib, hx, hx + to_sib, hy, hy + to_sib, hd, hd + to_sib)

    def weight_copy(which, index):
        columns = pl.ds(pl.multiple_of(index * width, width), width)
        source = (gate_hbm, up_hbm, down_hbm)[which]
        return pltpu.make_async_copy(
            source.at[:, columns], weights.at[which, index], weight_sem.at[which, index]
        )

    def fetch_weights(indices):
        for index in indices:
            for which in range(3):
                weight_copy(which, index).start()

    fetch_weights(order[:2])
    pending = []

    def start(source, target, send_sem, recv_sem, device):
        pltpu.make_async_remote_copy(
            src_ref=source,
            dst_ref=target,
            send_sem=send_sem,
            recv_sem=recv_sem,
            device_id=device,
            device_id_type=MESH,
        ).start()

    def send(source, target, send_sem, recv_sem, device):
        start(source, target, send_sem, recv_sem, device)
        pending.append((source, send_sem))

    def arrived(target, send_sem, recv_sem):
        pltpu.make_async_remote_copy(
            src_ref=target,
            dst_ref=target,
            send_sem=send_sem,
            recv_sem=recv_sem,
            device_id=at_hidden(sib),
            device_id_type=MESH,
        ).wait_recv()

    block_row = lax.broadcasted_iota(jnp.int32, (8, rows), 0)
    owner_of = jnp.full((8, rows), -1, jnp.int32)
    for j, owner in enumerate(owners):
        owner_of = jnp.where(block_row == j, owner, owner_of)
    small = in_ref[2 * rows : 2 * rows + 16, 0:LANES].astype(F32)[:, 0:rows]
    route_rows = small[0:2, :].astype(jnp.int32)
    first = jnp.broadcast_to(route_rows[0:1, :], (8, rows))
    second = jnp.broadcast_to(route_rows[1:2, :], (8, rows))
    prob_rows = small[2:4, :]
    match = (owner_of == first) | (owner_of == second)
    earlier = lax.broadcasted_iota(jnp.int32, (rows, rows), 0) < lax.broadcasted_iota(
        jnp.int32, (rows, rows), 1
    )
    rank = dot(match.astype(F32).astype(BF16), earlier.astype(F32).astype(BF16), NN)
    rank = jnp.where(match, rank, -1.0)
    block_prob = jnp.where(owner_of == first, jnp.broadcast_to(prob_rows[0:1, :], (8, rows)), 0.0)
    block_prob = block_prob + jnp.where(
        owner_of == second, jnp.broadcast_to(prob_rows[1:2, :], (8, rows)), 0.0
    )
    for j in range(dp_count):
        aux_send[j] = jnp.zeros((8, LANES), F32)
        aux_send[j, 0:1, 0:rows] = rank[j : j + 1, :]
        aux_send[j, 1:2, 0:rows] = block_prob[j : j + 1, :]
    wide_rank = jnp.concatenate([rank] * groups, axis=1)
    pack_row = lax.broadcasted_iota(jnp.int32, (packed, LANES), 0)
    pack_group = steps_of(pack_row, CAP, groups)
    pack_slot = (pack_row - CAP * pack_group).astype(F32)
    lane_group = steps_of(lax.broadcasted_iota(jnp.int32, (packed, LANES), 1), rows, groups)
    same_group = pack_group == lane_group
    select = jnp.concatenate(
        [
            jnp.where(
                same_group & (pack_slot == jnp.broadcast_to(wide_rank[j : j + 1, :], pack_slot.shape)),
                1.0,
                0.0,
            )
            for j in range(dp_count)
        ],
        axis=0,
    ).astype(BF16)

    for a in range(2):
        values = in_ref[a * rows : (a + 1) * rows, :]
        stacked = jnp.concatenate(
            [values[:, n * LANES : (n + 1) * LANES] for n in range(groups)], axis=0
        )
        zsend[a] = dot(select, stacked, NN).astype(BF16).reshape(dp_count, packed, LANES)
        zrecv[a, plane] = zsend[a, plane]
        if a == 0:
            aux_recv[plane] = aux_send[plane]
            pl.semaphore_wait(barrier, 4 + dp_count - 1)
        for step in range(1, dp_count):
            other, device = at_plane(step)
            send(
                zsend.at[a, other],
                zrecv.at[a, plane],
                z_send_sem.at[a, step],
                z_recv_sem.at[a, plane],
                device,
            )
    for step in range(1, dp_count):
        other, device = at_plane(step)
        send(
            aux_send.at[other],
            aux_recv.at[plane],
            aux_send_sem.at[step],
            aux_recv_sem.at[plane],
            device,
        )

    fetch_weights(order[2:6])

    def shift_of(shape, axis):
        slot = lax.broadcasted_iota(jnp.int32, shape, axis)
        return slot, slot + (packed - CAP) * steps_of(slot, CAP, dp_count)

    slot_index, slot_base = shift_of((slots, dp_count * packed), 0)
    packed_index = lax.broadcasted_iota(jnp.int32, (slots, dp_count * packed), 1)
    unpack = [
        jnp.where(packed_index == slot_base + CAP * n, 1.0, 0.0).astype(BF16) for n in range(groups)
    ]
    for a in range(2):
        for step in range(1, dp_count):
            other = (plane + step) % dp_count
            arrived(zrecv.at[a, other], z_send_sem.at[a, step], z_recv_sem.at[a, other])
        received = zrecv[a].reshape(dp_count * packed, LANES)
        for n in range(groups):
            xbuf[a, h, :, n * LANES : (n + 1) * LANES] = dot(unpack[n], received, NN).astype(BF16)
        for slot, partner in enumerate((hx, hy, sib)):
            send(
                xbuf.at[a, h],
                xbuf.at[a, h],
                x_send.at[a, slot],
                x_recv.at[a, h],
                at_hidden(partner),
            )

    fetch_weights(order[6:])

    def wait_x(a, index):
        arrived(xbuf.at[a, index], x_send.at[a, 0], x_recv.at[a, index])

    def forward(a, index, partner, slot):
        start(
            xbuf.at[a, index],
            xbuf.at[a, index],
            x_send.at[a, slot],
            x_recv.at[a, index],
            at_hidden(partner),
        )

    acc[...] = jnp.zeros_like(acc)

    @pl.loop(0, 8)
    def _(i):
        @pl.when(i == 1)
        def _():
            wait_x(0, hx)
            forward(0, hx, hy, 3)
            forward(0, hx, sib, 4)
            wait_x(0, hy)
            forward(0, hy, sib, 5)
            wait_x(0, sib)
            wait_x(1, sib)

        @pl.when(i == 2)
        def _():
            wait_x(1, hy)
            forward(1, hy, hx, 3)
            forward(1, hy, sib, 4)
            wait_x(1, hx)
            forward(1, hx, sib, 5)

        @pl.when(i == 3)
        def _():
            wait_x(0, hx + to_sib)
            wait_x(1, hx + to_sib)

        @pl.when(i == 5)
        def _():
            wait_x(0, hd)
            forward(0, hd, sib, 6)
            wait_x(1, hd)
            forward(1, hd, sib, 6)
            wait_x(0, hy + to_sib)
            wait_x(1, hy + to_sib)

        @pl.when(i == 7)
        def _():
            wait_x(0, hd + to_sib)
            wait_x(1, hd + to_sib)

        index = chip_at((i // 2) % 2, i // 4) + (i % 2) * to_sib
        for which in range(3):
            weight_copy(which, index).wait()
            left = xbuf[0 if which < 2 else 1, index]
            for begin, size in strips(units, 2 * LANES):
                acc[which, :, begin : begin + size] += dot(
                    left, weights[which, index, begin : begin + size, :], NT
                )

    x_copy = pltpu.make_async_copy(xbuf.at[0], x_out, out_sem.at[0])
    x_copy.start()

    for step in range(1, dp_count):
        other = (plane + step) % dp_count
        arrived(aux_recv.at[other], aux_send_sem.at[step], aux_recv_sem.at[other])
    slot_value = lax.broadcasted_iota(jnp.int32, (slots, rows), 0).astype(F32)
    slot_prob = jnp.zeros((slots, 1), F32)
    for source in range(dp_count):
        source_rank = jnp.broadcast_to(aux_recv[source, 0:1, 0:rows], (slots, rows))
        source_prob = jnp.broadcast_to(aux_recv[source, 1:2, 0:rows], (slots, rows))
        hit = (source_rank >= 0.0) & (slot_value == source_rank + float(CAP * source))
        slot_prob = slot_prob + jnp.sum(jnp.where(hit, source_prob, 0.0), axis=1, keepdims=True)

    slot_prob = jnp.broadcast_to(slot_prob, (slots, LANES))
    router_sum[...] = jnp.zeros_like(router_sum)

    @pl.loop(0, units // LANES)
    def _(i):
        part = pl.ds(pl.multiple_of(i * LANES, LANES), LANES)
        gate_pre = acc[0, :, part]
        up_pre = acc[1, :, part]
        back_pre = acc[2, :, part]
        sigmoid_gate = jax.nn.sigmoid(gate_pre)
        silu_gate = gate_pre * sigmoid_gate
        scaled = slot_prob * back_pre
        dbuf[0, :, part] = (
            scaled * up_pre * sigmoid_gate * (1.0 + gate_pre * (1.0 - sigmoid_gate))
        ).astype(BF16)
        dbuf[1, :, part] = (scaled * silu_gate).astype(BF16)
        router_sum[...] += silu_gate * up_pre * back_pre

    d_copy = pltpu.make_async_copy(dbuf, d_out, out_sem.at[1])
    d_copy.start()
    router = jnp.broadcast_to(jnp.sum(router_sum[...], axis=1, keepdims=True), (slots, LANES))
    if slots < LANES:
        router = jnp.concatenate([router, jnp.zeros((LANES - slots, LANES), F32)], axis=0)
    q_send[0] = router.T[0:8, :]
    send(q_send.at[0], q_recv.at[0], q_send_sem.at[0], q_recv_sem.at[0], at_hidden(sib))

    column_strips = strips(width, 2 * LANES)

    def partial(index, begin, size):
        part = slice(begin, begin + size)
        return dot(dbuf[0], weights[0, index, :, part], NN) + dot(
            dbuf[1], weights[1, index, :, part], NN
        )

    def chip_of(slot):
        return chip_at((3 - slot) // 2, (3 - slot) % 2)

    @pl.loop(0, 5)
    def _(turn):
        @pl.when(turn < 4)
        def _():
            for begin, size in column_strips:
                one_send[turn, :, begin : begin + size] = partial(
                    chip_of(turn) + to_sib, begin, size
                ).astype(BF16)
            start(
                one_send.at[turn],
                one_recv.at[turn],
                one_send_sem.at[turn],
                one_recv_sem.at[turn],
                at_hidden(sib),
            )

        @pl.when(turn == 1)
        def _():
            arrived(q_recv.at[0], q_send_sem.at[0], q_recv_sem.at[0])
            q_send[1] = q_send[0] + q_recv[0]
            for place, index in enumerate((hd, hx, hy)):
                start(
                    q_send.at[1],
                    q_recv.at[1 + place],
                    q_send_sem.at[1 + place],
                    q_recv_sem.at[1 + place],
                    at_hidden(index),
                )

        @pl.when(turn > 0)
        def _():
            slot = turn - 1
            index = chip_of(slot)
            for begin, size in column_strips:
                own_part[:, begin : begin + size] = partial(index, begin, size)
            arrived(one_recv.at[slot], one_send_sem.at[slot], one_recv_sem.at[slot])
            own_part[...] += one_recv[slot].astype(F32)

            @pl.when(slot < 3)
            def _():
                two_send[slot] = own_part[...].astype(BF16)
                start(
                    two_send.at[slot],
                    two_recv.at[slot],
                    two_send_sem.at[slot],
                    two_recv_sem.at[slot],
                    at_hidden(index),
                )

    for a in range(2):
        for slot in range(3, 7):
            pending.append((xbuf.at[a, h], x_send.at[a, slot]))
    for slot in range(3):
        pending.append((q_send.at[1], q_send_sem.at[1 + slot]))
    for slot in range(4):
        pending.append((one_send.at[slot], one_send_sem.at[slot]))
    for slot in range(3):
        pending.append((two_send.at[slot], two_send_sem.at[slot]))

    for slot in range(3):
        arrived(q_recv.at[1 + slot], q_send_sem.at[1 + slot], q_recv_sem.at[1 + slot])
    q_total = (q_send[1] + q_recv[2]) + (q_recv[3] + q_recv[1])
    qz_send[...] = q_total
    qz_recv[plane] = q_total
    for step in range(1, dp_count):
        _, device = at_plane(step)
        send(qz_send, qz_recv.at[plane], qz_send_sem.at[step], qz_recv_sem.at[plane], device)

    for slot in range(3):
        arrived(two_recv.at[slot], two_send_sem.at[slot], two_recv_sem.at[slot])
    features = (
        own_part[...]
        + two_recv[0].astype(F32)
        + two_recv[1].astype(F32)
        + two_recv[2].astype(F32)
    ).astype(BF16)
    _, slot_base = shift_of((dp_count * packed, slots), 1)
    packed_index = lax.broadcasted_iota(jnp.int32, (dp_count * packed, slots), 0)
    returned = jnp.zeros((dp_count * packed, LANES), F32)
    for n in range(groups):
        place = jnp.where(packed_index == slot_base + CAP * n, 1.0, 0.0).astype(BF16)
        returned = returned + dot(place, features[:, n * LANES : (n + 1) * LANES], NN)
    back_send[...] = returned.astype(BF16).reshape(dp_count, packed, LANES)
    back_recv[plane] = back_send[plane]
    for step in range(1, dp_count):
        other, device = at_plane(step)
        send(
            back_send.at[other],
            back_recv.at[plane],
            back_send_sem.at[step],
            back_recv_sem.at[plane],
            device,
        )

    for step in range(1, dp_count):
        other = (plane + step) % dp_count
        arrived(qz_recv.at[other], qz_send_sem.at[step], qz_recv_sem.at[other])
    q_rows = jnp.concatenate(
        [qz_recv[j, 0:1, :] for j in range(dp_count)] + [jnp.zeros((LANES - dp_count, LANES), F32)],
        axis=0,
    )
    q_columns = q_rows.T
    wanted = lax.broadcasted_iota(jnp.int32, (LANES, rows), 0).astype(F32) - (CAP * plane).astype(F32)
    found = [jnp.zeros((1, rows), F32), jnp.zeros((1, rows), F32)]
    for j, owner in enumerate(owners):
        hit = (wanted == jnp.broadcast_to(rank[j : j + 1, :], wanted.shape)) & (wanted >= 0.0)
        column = jnp.broadcast_to(q_columns[:, j : j + 1], wanted.shape)
        value = jnp.sum(jnp.where(hit, column, 0.0), axis=0, keepdims=True)
        for k in range(2):
            found[k] = found[k] + jnp.where(route_rows[k : k + 1, :] == owner, value, 0.0)
    grad_probs_ref[...] = jnp.concatenate(found, axis=0)

    for step in range(1, dp_count):
        other = (plane + step) % dp_count
        arrived(back_recv.at[other], back_send_sem.at[step], back_recv_sem.at[other])
    stacked = dot(select, back_recv[...].reshape(dp_count * packed, LANES), TN)
    for n in range(groups):
        grad_tokens_ref[:, n * LANES : (n + 1) * LANES] = stacked[n * rows : (n + 1) * rows, :].astype(
            BF16
        )

    for source, send_sem in pending:
        pltpu.make_async_remote_copy(
            src_ref=source,
            dst_ref=source,
            send_sem=send_sem,
            recv_sem=send_sem,
            device_id=at_hidden(sib),
            device_id_type=MESH,
        ).wait_send()
    x_copy.wait()
    d_copy.wait()


def outer_kernel(d_ref, x_ref, tokens_ref, probs_ref, gate_ref, up_ref, tokens_out, probs_out):
    width = x_ref.shape[2]
    for which, out in enumerate((gate_ref, up_ref)):
        left = d_ref[which].astype(F32).T.astype(BF16)
        for index in range(x_ref.shape[0]):
            for begin, size in strips(width, 2 * LANES):
                start = index * width + begin
                out[:, start : start + size] = dot(
                    left, x_ref[index, :, begin : begin + size], NN
                ).astype(BF16)

    @pl.when(pl.program_id(0) == 0)
    def _():
        tokens_out[...] = tokens_ref[...]
        probs_out[...] = probs_ref[...]


def fused_body(dp_count, tokens, grad_out, routes, probs, gate_weight, up_weight, down_weight):
    rows, width = tokens.shape
    units, model = gate_weight.shape
    hidden_count = model // width
    groups = width // LANES
    packed = CAP * groups
    slots = CAP * dp_count
    large_count = dp_count // 6
    owners = tuple(j // 4 if j < 4 * large_count else j - 3 * large_count for j in range(dp_count))
    dma = pltpu.SemaphoreType.DMA
    vmem = pl.BlockSpec(memory_space=pltpu.VMEM)
    anywhere = pl.BlockSpec(memory_space=pl.ANY)
    packed_in = sum(
        jnp.pad(
            part.astype(BF16),
            ((first, 2 * rows + 16 - first - part.shape[0]), (0, width - part.shape[1])),
        )
        for first, part in (
            (0, tokens),
            (rows, grad_out),
            (2 * rows, routes.T),
            (2 * rows + 2, probs.T),
        )
    )
    grad_tokens, grad_probs, x_all, d_all = pl.pallas_call(
        functools.partial(fused_kernel, dp_count, owners),
        out_shape=(
            jax.ShapeDtypeStruct((rows, width), BF16),
            jax.ShapeDtypeStruct((2, rows), F32),
            jax.ShapeDtypeStruct((hidden_count, slots, width), BF16),
            jax.ShapeDtypeStruct((2, slots, units), BF16),
        ),
        in_specs=[vmem] + [anywhere] * 3,
        out_specs=(vmem, vmem, anywhere, anywhere),
        scratch_shapes=[
            pltpu.VMEM((3, hidden_count, units, width), BF16),
            dma((3, hidden_count)),
            pltpu.VMEM((2, hidden_count, slots, width), BF16),
            dma((2, 7)),
            dma((2, hidden_count)),
            pltpu.VMEM((2, dp_count, packed, LANES), BF16),
            pltpu.VMEM((2, dp_count, packed, LANES), BF16),
            dma((2, dp_count)),
            dma((2, dp_count)),
            pltpu.VMEM((dp_count, 8, LANES), F32),
            pltpu.VMEM((dp_count, 8, LANES), F32),
            dma((dp_count,)),
            dma((dp_count,)),
            pltpu.VMEM((3, slots, units), F32),
            pltpu.VMEM((slots, LANES), F32),
            pltpu.VMEM((2, slots, units), BF16),
            pltpu.VMEM((4, slots, width), BF16),
            pltpu.VMEM((4, slots, width), BF16),
            dma((4,)),
            dma((4,)),
            pltpu.VMEM((3, slots, width), BF16),
            pltpu.VMEM((3, slots, width), BF16),
            dma((3,)),
            dma((3,)),
            pltpu.VMEM((slots, width), F32),
            pltpu.VMEM((2, 8, LANES), F32),
            pltpu.VMEM((4, 8, LANES), F32),
            dma((4,)),
            dma((4,)),
            pltpu.VMEM((dp_count, packed, LANES), BF16),
            pltpu.VMEM((dp_count, packed, LANES), BF16),
            dma((dp_count,)),
            dma((dp_count,)),
            pltpu.VMEM((8, LANES), F32),
            pltpu.VMEM((dp_count, 8, LANES), F32),
            dma((dp_count,)),
            dma((dp_count,)),
            dma((2,)),
        ],
        compiler_params=pltpu.CompilerParams(
            collective_id=0, has_side_effects=True, vmem_limit_bytes=48 << 20
        ),
    )(packed_in, gate_weight, up_weight, down_weight)
    grad_gate, grad_up, grad_tokens, grad_probs = pl.pallas_call(
        outer_kernel,
        grid=(units // LANES,),
        out_shape=(
            jax.ShapeDtypeStruct((units, model), BF16),
            jax.ShapeDtypeStruct((units, model), BF16),
            jax.ShapeDtypeStruct((rows, width), BF16),
            jax.ShapeDtypeStruct((2, rows), F32),
        ),
        in_specs=[
            pl.BlockSpec((2, slots, LANES), lambda i: (0, 0, i)),
            pl.BlockSpec((hidden_count, slots, width), lambda i: (0, 0, 0)),
            pl.BlockSpec((rows, width), lambda i: (0, 0)),
            pl.BlockSpec((2, rows), lambda i: (0, 0)),
        ],
        out_specs=(
            pl.BlockSpec((LANES, model), lambda i: (i, 0)),
            pl.BlockSpec((LANES, model), lambda i: (i, 0)),
            pl.BlockSpec((rows, width), lambda i: (0, 0)),
            pl.BlockSpec((2, rows), lambda i: (0, 0)),
        ),
        compiler_params=pltpu.CompilerParams(vmem_limit_bytes=48 << 20),
    )(d_all, x_all, grad_tokens, grad_probs)
    return (grad_tokens, grad_probs.T, grad_gate, grad_up)


def solution(mesh):
    placed = (
        P("dp", "hidden"),
        P("dp", "hidden"),
        P("dp", None),
        P("dp", None),
        P(("dp", "hidden"), None),
        P(("dp", "hidden"), None),
        P(("dp", "hidden"), None),
    )

    def local(tokens, grad_out, routes, probs, gate_weight, up_weight, down_weight):
        args = (tokens, grad_out, routes, probs, gate_weight, up_weight, down_weight)
        if fits(mesh.shape["dp"], mesh.shape["hidden"], tokens.shape, gate_weight.shape):
            return fused_body(mesh.shape["dp"], *args)
        return body(*args)

    return jax.shard_map(
        local,
        mesh=mesh,
        in_specs=placed,
        out_specs=(
            P("dp", "hidden"),
            P("dp", None),
            P(("dp", "hidden"), None),
            P(("dp", "hidden"), None),
        ),
        check_vma=False,
    )
```
